32 devices in a mesh: groups: 2 (over x), blk: 4 (over y, core), row: 4 (over z).
Axes of the slice: x: 2, y: 2, z: 4, core: 2. Of those that a mesh axis runs over, the one named last changes fastest.
Arguments:
- coords: float32 [3, 24576], P(None, ('groups', 'blk', 'row')), parts along dimension 1, may hold values from 0 to 1
- charges: float32 [24576], P(('groups', 'blk', 'row')), parts along dimension 0, may hold values from -1 to 1
- counts: int32 [32], P(('groups', 'blk', 'row')), parts along dimension 0, may hold values from 256 to 768, as said below
- send_slot: int32 [24576], P(('groups', 'blk', 'row')), parts along dimension 0, may hold values from 0 to 1023, as said below
- recv_index: int32 [16384], P(('groups', 'blk', 'row')), parts along dimension 0, may hold values from 0 to 1023, as said below
- wave_ints: int32 [3, 24576], P(None, 'blk'), may hold values from -36 to 36, as said below
Outputs:
- slot_forces: float32 [3, 24576], P(None, ('groups', 'blk', 'row')), parts along dimension 1
- atom_forces: float32 [3, 16384], P(None, ('groups', 'blk', 'row')), parts along dimension 1
The draws below stay inside these ranges and needn't reach their ends.
There are 2 independent parts, one for each index of `groups`. The reference program is written for one: setup_inputs(seed, part) draws one part's arguments, and reference() takes and returns one part's arrays. A program takes and returns all parts, laid end to end along the dimension named above; an argument that names none is the same for every part. Nothing has to cross between parts.
Inputs may be any that keep to these rules, and one draw needn't show every extreme that they name: The counts of one system sum to 8192; the largest is 768. `send_slot`: for a live slot the value is d * 64 + r: the ion goes to k-space device d as its r-th arrival from this owner. Live values of one owner are distinct, and the ranks r to one device are 0 up to the number sent there minus one. Every device receives exactly 512 ions; some owner sends exactly 64 to some device. Slots that are not live hold arbitrary values. `recv_index`: the 512 values of device d are distinct and are exactly the arrivals s * 64 + r sent to d. `wave_ints`: each column is (h, k, l) with |h|, |k| at most 12 and l nonzero.
All inputs are finite; a program needn't handle non-finite values.
Results may differ from the reference program's by a relative error of at most 0.00007.
Values sent between devices are 32-bit elements; how exact they have to be, the bound alone decides.
A program may use at most 128 MiB of HBM per device.

```python
import math
import jax
import jax.numpy as jnp
from jax import lax

A_DEV = 512
K = 24576
HMAX = 12
LMAX = 36
PEERS = 16
SLOTS_DEV = 768
ION_SLOT_TOTAL = 12288
PAIR_CAP = 64


def balanced_loads(sub_key, half_load):
    pair_count = PEERS // 2
    key_swing, key_order = jax.random.split(sub_key)
    swing = jax.random.randint(key_swing, (pair_count,), -half_load, half_load + 1)
    swing = swing.at[0].set(half_load)
    loads = jnp.stack([half_load + swing, half_load - swing], axis=1).reshape(-1)
    order = jax.random.permutation(key_order, PEERS)
    return loads[order].astype(jnp.int32)


def routing_tables(key):
    base = jax.random.fold_in(key, 7)
    keys = jax.random.split(base, 5)
    half_load = A_DEV // (2 * PEERS)
    owner_load = balanced_loads(keys[0], half_load)
    shared_load = balanced_loads(keys[1], half_load)
    peer_ids = jnp.arange(PEERS, dtype=jnp.int32)
    shifted = (peer_ids[:, None] + peer_ids[None, :]) % PEERS
    sent = owner_load[:, None] + shared_load[shifted]
    counts = jnp.sum(sent, axis=1).astype(jnp.int32)
    flat_ids = jnp.arange(PEERS * PAIR_CAP, dtype=jnp.int32)
    ranks = flat_ids % PAIR_CAP
    partner = flat_ids // PAIR_CAP

    def owner_slots(sub_key, owner):
        usable = ranks < sent[owner, partner]
        scores = jnp.where(usable, jax.random.permutation(sub_key, PEERS * PAIR_CAP).astype(jnp.int32), PEERS * PAIR_CAP + flat_ids)
        return jnp.argsort(scores, stable=True)[:SLOTS_DEV].astype(jnp.int32)
    send_keys = jax.random.split(keys[2], PEERS)
    outbound_rows = jax.vmap(owner_slots)(send_keys, peer_ids)
    slot_ids = jnp.arange(SLOTS_DEV, dtype=jnp.int32)
    filler = jax.random.randint(keys[3], (PEERS, SLOTS_DEV), 0, PEERS * PAIR_CAP)
    send_slot = jnp.where(slot_ids[None, :] < counts[:, None], outbound_rows, filler).reshape(-1).astype(jnp.int32)

    def device_rows(sub_key, device):
        usable = ranks < sent[partner, device]
        scores = jnp.where(usable, jax.random.permutation(sub_key, PEERS * PAIR_CAP).astype(jnp.int32), PEERS * PAIR_CAP + flat_ids)
        return jnp.argsort(scores, stable=True)[:A_DEV].astype(jnp.int32)
    recv_keys = jax.random.split(keys[4], PEERS)
    recv_index = jax.vmap(device_rows)(recv_keys, peer_ids).reshape(-1).astype(jnp.int32)
    return (counts, send_slot, recv_index)


def draw_counts(key, part):
    return routing_tables(key)[0]


def draw_send_slot(key, part):
    return routing_tables(key)[1]


def draw_recv_index(key, part):
    return routing_tables(key)[2]


def draw_wave_ints(key, part):
    keys = jax.random.split(jax.random.fold_in(key, 11), 4)
    first = jax.random.randint(keys[0], (K,), -HMAX, HMAX + 1)
    second = jax.random.randint(keys[1], (K,), -HMAX, HMAX + 1)
    third = jax.random.randint(keys[2], (K,), 1, LMAX + 1)
    signs = 2 * jax.random.randint(keys[3], (K,), 0, 2) - 1
    triples = jnp.stack([first, second, third * signs]).astype(jnp.int32)
    triples = triples.at[:, 0].set(jnp.array([HMAX, -HMAX, LMAX], jnp.int32))
    triples = triples.at[:, 1].set(jnp.array([-HMAX, HMAX, -LMAX], jnp.int32))
    return triples


def block_levels(rng, shape, cuts, least, top_value):
    level, own = 1.0, jax.random.fold_in(rng, 6)
    for dim, blocks in cuts:
        steps = jnp.exp(jax.random.uniform(jax.random.fold_in(own, dim), (blocks,), jnp.float32, least / len(cuts), top_value / len(cuts)))
        level = level * jnp.repeat(steps, shape[dim] // blocks).reshape([-1 if axis == dim else 1 for axis in range(len(shape))])
    return level


def setup_inputs(seed: int = 0, part: int = 0) -> dict:
    key_list = jax.random.split(jax.random.key(seed), 7)
    own_keys = jax.random.split(jax.random.fold_in(key_list[6], part), 7)
    return {
        "coords": jnp.clip(1.0 * jax.random.uniform(own_keys[0], (3, ION_SLOT_TOTAL), jnp.float32) ** block_levels(own_keys[0], (3, ION_SLOT_TOTAL), ((1, 16),), -0.2, 0.2), 0.0, 1.0),
        "charges": jnp.clip(jax.random.uniform(own_keys[1], (ION_SLOT_TOTAL,), jnp.float32, -1.0, 1.0) * block_levels(own_keys[1], (ION_SLOT_TOTAL,), ((0, 16),), -0.4, 0.0), -1.0, 1.0),
        "counts": draw_counts(jax.random.fold_in(jax.random.fold_in(key_list[6], part), 71), part),
        "send_slot": draw_send_slot(jax.random.fold_in(jax.random.fold_in(key_list[6], part), 71), part),
        "recv_index": draw_recv_index(jax.random.fold_in(jax.random.fold_in(key_list[6], part), 71), part),
        "wave_ints": draw_wave_ints(jax.random.fold_in(key_list[6], 71), part),
    }


DOUBLE_PI = 2.0 * math.pi
EWALD_BETA = 30.0
BOX_Z = 3.0
FORCE_GAIN = 400.0

def phys_vectors(wave_float):
    return jnp.stack([DOUBLE_PI * wave_float[0], DOUBLE_PI * wave_float[1], DOUBLE_PI * wave_float[2] / BOX_Z])

def phase_angles(wave_float, frac):
    inner = wave_float[0][:, None] * frac[0][None, :] + wave_float[1][:, None] * frac[1][None, :]
    inner = inner + wave_float[2][:, None] * frac[2][None, :]
    return DOUBLE_PI * inner

def pull_sum(wave_float, cos_weighted, sin_weighted, frac):
    angles = phase_angles(wave_float, frac)
    coef = jnp.sin(angles) * cos_weighted[:, None] - jnp.cos(angles) * sin_weighted[:, None]
    wave_phys = phys_vectors(wave_float)
    return lax.optimization_barrier(jnp.sum(wave_phys[:, :, None] * coef[None, :, :], axis=1))

def reference(coords, charges, counts, send_slot, recv_index, wave_ints):
    devices = counts.shape[0]
    slots_dev = charges.shape[0] // devices
    atoms_dev = recv_index.shape[0] // devices
    pair_cap = 2 * atoms_dev // devices
    buf_width = devices * pair_cap
    slot_ids = jnp.arange(slots_dev, dtype=jnp.int32)
    is_live = slot_ids[None, :] < counts[:, None]
    source = jnp.arange(devices, dtype=jnp.int32)[:, None]
    target_slot = jnp.where(is_live, source * buf_width + send_slot.reshape(devices, slots_dev), devices * buf_width)
    target_slot = target_slot.reshape(-1).astype(jnp.int32)
    value_entries = jnp.concatenate([coords, charges[None, :]], axis=0)
    table = jnp.zeros((4, devices * buf_width), jnp.float32).at[:, target_slot].set(value_entries, mode='drop')
    dest = jnp.repeat(jnp.arange(devices, dtype=jnp.int32), atoms_dev)
    where_from = (recv_index // pair_cap * buf_width + dest * pair_cap + recv_index % pair_cap).astype(jnp.int32)
    atom_rows = table[:, where_from]
    n_total = atom_rows.shape[1]
    wave_float = wave_ints.astype(jnp.float32)
    k_block = 128
    k_blocks = wave_float.reshape(3, K // k_block, k_block).transpose(1, 0, 2)

    def block_sums(wave_part):
        angles = phase_angles(wave_part, atom_rows[:3])
        return (lax.optimization_barrier(jnp.sum(atom_rows[3][None, :] * jnp.cos(angles), axis=1)), lax.optimization_barrier(jnp.sum(atom_rows[3][None, :] * jnp.sin(angles), axis=1)))
    cos_sum, sin_sum = lax.map(block_sums, k_blocks)
    cos_sum = cos_sum.reshape(-1)
    sin_sum = sin_sum.reshape(-1)
    wave_phys = phys_vectors(wave_float)
    k_squared = lax.optimization_barrier(jnp.sum(wave_phys * wave_phys, axis=0))
    weight = jnp.exp(-k_squared / (4.0 * EWALD_BETA * EWALD_BETA)) / k_squared
    cos_weighted = weight * cos_sum
    sin_weighted = weight * sin_sum
    force_scale = FORCE_GAIN / math.sqrt(float(n_total * K))
    a_block = 1024
    atom_blocks = atom_rows.reshape(4, n_total // a_block, a_block).transpose(1, 0, 2)

    def force_of_block(block_rows):
        pull_total = pull_sum(wave_float, cos_weighted, sin_weighted, block_rows[:3])
        return force_scale * block_rows[3][None, :] * pull_total
    atom_forces = lax.map(force_of_block, atom_blocks).transpose(1, 0, 2).reshape(3, n_total)
    back = jnp.zeros((3, devices * buf_width), jnp.float32).at[:, where_from].set(atom_forces)
    picked = back[:, jnp.minimum(target_slot, devices * buf_width - 1)]
    slot_forces = jnp.where(is_live.reshape(-1)[None, :], picked, 0.0)
    return (slot_forces, atom_forces)
```

```python
import functools
import math

import jax
import jax.numpy as jnp
import numpy as np
from jax import lax
from jax.experimental import pallas as pl
from jax.experimental.pallas import tpu as pltpu
from jax.sharding import PartitionSpec as P

EWALD_BETA = 30.0
BOX_Z = 3.0
FORCE_GAIN = 400.0
HMAX = 12
LMAX = 36
L_ROWS = 40
QUADS = 160
REGULAR = HMAX * HMAX
WAVES = 4 * QUADS
W_TILES = WAVES // 128
H_TILES = L_ROWS // 8 * W_TILES
T_TILES = 2 * H_TILES
F32 = jnp.float32
BF16 = jnp.bfloat16
NT = (((1,), (1,)), ((), ()))
NN = (((1,), (0,)), ((), ()))
TWO_PI = 2.0 * math.pi


def fit(f, terms):
    n = 64
    u = 0.125 + 0.125 * np.cos((2 * np.arange(n) + 1) * np.pi / (2 * n))
    c = np.polynomial.chebyshev.Chebyshev.fit(u, f(np.sqrt(u)), terms - 1, domain=[0.0, 0.25])
    return [float(v) for v in c.convert(kind=np.polynomial.Polynomial).coef]


SIN_C = fit(lambda r: np.sin(np.pi * r) / r, 5)
COS_C = fit(lambda r: np.cos(np.pi * r), 5)


def iota(shape, dim):
    return lax.broadcasted_iota(jnp.int32, shape, dim)


def horner(coefs, u):
    out = u * coefs[-1] + coefs[-2]
    for c in coefs[-3::-1]:
        out = out * u + c
    return out


def turns(mult, frac):
    t = mult * frac
    r = t - jnp.floor(t + 0.5)
    u = r * r
    s = r * horner(SIN_C, u)
    c = horner(COS_C, u)
    twice = s + s
    return 1.0 - twice * s, twice * c


def split2(x):
    hi = x.astype(BF16)
    return hi, (x - hi.astype(F32)).astype(BF16)


def split3(x):
    hi = x.astype(BF16)
    rest = x - hi.astype(F32)
    mid = rest.astype(BF16)
    return hi, mid, (rest - mid.astype(F32)).astype(BF16)


def mm(a, b, dims):
    return lax.dot_general(a, b, dims, preferred_element_type=F32)


def mm3(x, picks, dims):
    rows = x.shape[0]
    out = mm(jnp.concatenate(split3(x)), picks, dims)
    return out[:rows] + out[rows : 2 * rows] + out[2 * rows :]


def quad_of(h, k):
    even = jnp.where(k <= 8, 8 * h + k - 9, 83 + 4 * h + k)
    lone = jnp.where(h + k == 0, REGULAR + HMAX, REGULAR - 1 + h + k)
    return jnp.where((h > 0) & (k > 0), even, lone)


def lane_waves():
    lane = iota((1, WAVES), 1)
    block = (lane >> 5) & 3
    quad = ((lane >> 7) << 5) + (lane & 31)
    late = quad - 96
    h = jnp.where(quad < 96, (quad >> 3) + 1, (late >> 2) + 1)
    k = jnp.where(quad < 96, (quad & 7) + 1, (late & 3) + 9)
    lone = jnp.where(quad < REGULAR + HMAX, quad - (REGULAR - 1), 0)
    regular = quad < REGULAR
    odd = (block & 1) == 1
    h = jnp.where(regular, h, jnp.where(odd, 0, lone))
    k = jnp.where(regular, k, jnp.where(odd, lone, 0))
    return h.astype(F32), k.astype(F32), block, regular


def fill_plane(frac_x, frac_y, hi, lo):
    width = frac_x.shape[1]
    row = iota((16, 1), 0)
    mult = jnp.where(row < 12, row + 1, row - 3).astype(F32)
    cx, sx = turns(mult, frac_x)
    cy, sy = turns(mult, frac_y)
    low = iota((8, width), 0) < 4

    def two(v, i):
        a = jnp.broadcast_to(v[i : i + 1], (8, width))
        return jnp.where(low, a, jnp.broadcast_to(v[i + 1 : i + 2], (8, width)))

    def unit(u):
        if u < HMAX:
            a, b = cx[u : u + 1], sx[u : u + 1]
            c, d = cy[:8], sy[:8]
        elif u < 18:
            i = 2 * (u - HMAX)
            a, b = two(cx, i), two(sx, i)
            c, d = cy[8:], sy[8:]
        elif u == 18:
            return cx[:8], cy[:8], sx[:8], sy[:8]
        else:
            return jnp.where(low, cx[8:], 1.0), cy[8:], jnp.where(low, sx[8:], 0.0), sy[8:]
        return a * c, b * d, b * c, a * d

    for t in range(W_TILES):
        units = [unit(4 * t + i) for i in range(4)]
        for block in range(4):
            value = jnp.concatenate([v[block] for v in units])
            place = pl.ds(128 * t + 32 * block, 32)
            hi[place, :], lo[place, :] = split2(value)


def column(frac_z, gain=None):
    c, s = turns((iota((8, 1), 0) + 1).astype(F32), frac_z)
    c8, s8 = c[7:8], s[7:8]
    if gain is not None:
        c, s = c * gain, s * gain
    cs, ss = [c], [s]
    for _ in range(L_ROWS // 8 - 1):
        c, s = c * c8 - s * s8, s * c8 + c * s8
        cs.append(c)
        ss.append(s)
    return jnp.concatenate(cs + ss)


def sums_of(v, hi, lo):
    vh, vl = split2(v)
    out = mm(jnp.concatenate([vh, vl]), hi, NT)
    return out[: 2 * L_ROWS] + out[2 * L_ROWS :] + mm(vh, lo, NT)


def each(count, f):
    if count <= 16:
        for o in range(1, count):
            f(o)
    else:
        pl.loop(1, count)(f)


def kernel(
    blks, rows, cap, scale,
    coords_in, charges_in, counts_in, send_in, recv_in, wave_in,
    forces,
    coords, charges, counts, send_slot, recv_index, wave,
    table, even, odd, ion, got_ion, mail, got_mail,
    hist, hist_sib, hist_chip, got_hist, acc, sums, from_sib,
    in_s, i_s, i_r, m_s, m_r, h_s, h_r, y_s, y_r, x_s, x_r,
):
    devices = blks * rows
    chips = devices // 2
    ys = blks // 2
    slots = coords.shape[1]
    atoms = recv_index.shape[0]
    both = slots + atoms
    blk, row = lax.axis_index("blk"), lax.axis_index("row")
    core = lax.rem(blk, 2)
    y = lax.div(blk, 2)
    me = blk * rows + row
    mesh_id = pl.DeviceIdType.MESH
    sibling = {"blk": blk + 1 - 2 * core, "row": row}

    loads = [
        pltpu.make_async_copy(src, dst, in_s.at[i])
        for i, (src, dst) in enumerate(
            (
                (coords_in, coords), (charges_in, charges), (counts_in, counts),
                (send_in, send_slot), (wave_in, wave), (recv_in, recv_index),
            )
        )
    ]
    for load in loads:
        load.start()

    blk_at = [lax.rem(blk + i, blks) for i in range(blks)]
    row_at = [lax.rem(row + i, rows) for i in range(rows)]

    def other(o):
        if isinstance(o, int):
            return {"blk": blk_at[o // rows], "row": row_at[o % rows]}
        return {"blk": lax.rem(blk + lax.div(o, rows), blks), "row": lax.rem(row + lax.rem(o, rows), rows)}

    def other_chip(o):
        if isinstance(o, int):
            return {"blk": blk_at[2 * (o // rows)], "row": row_at[o % rows]}
        return other(2 * rows * lax.div(o, rows) + lax.rem(o, rows))

    def copy(src, dst, s, r, o, dev):
        return pltpu.make_async_remote_copy(
            src_ref=src, dst_ref=dst, send_sem=s.at[o], recv_sem=r.at[o],
            device_id=dev, device_id_type=mesh_id,
        )

    def ion_copy(o):
        return copy(ion, got_ion.at[o], i_s, i_r, o, other_chip(o))

    def mail_copy(o):
        dev = other(o)
        return copy(mail.at[dev["blk"] * rows + dev["row"]], got_mail.at[o], m_s, m_r, o, dev)

    def hist_sib_copy():
        return copy(hist, hist_sib, h_s, h_r, 0, sibling)

    def hist_copy(o):
        return copy(hist_chip, got_hist.at[o], y_s, y_r, o, other_chip(o * rows))

    def sums_copy():
        return copy(sums, from_sib, x_s, x_r, 0, sibling)

    barrier = pltpu.get_barrier_semaphore()
    each(
        devices,
        lambda o: pl.semaphore_signal(
            barrier, inc=1, device_id=other(o), device_id_type=mesh_id
        ),
    )

    for load in loads[:3]:
        load.wait()
    live = iota((1, slots), 1) < jnp.broadcast_to(counts[...].reshape(1, 1), (1, slots))
    q = jnp.where(live, charges[...].reshape(1, slots), 0.0)
    ion[0:3] = coords[...]
    ion[3:4] = q
    pl.semaphore_wait(barrier, devices - 1)
    each(chips, lambda o: ion_copy(o).start())

    loads[3].wait()
    target = jnp.where(live, send_slot[...].reshape(1, slots), -1)
    spots = jnp.where(target == iota((devices * cap, slots), 0), 1.0, 0.0).astype(BF16)
    entries = jnp.concatenate([coords[...], q, jnp.zeros((4, slots), F32)])
    out = mm3(entries, spots, NT)
    per_tile = 128 // cap
    lane_part = iota((8, 128), 1) // cap
    for d in range(devices):
        tile = out[:, 128 * (d // per_tile) : 128 * (d // per_tile) + 128]
        tile = jnp.where(lane_part == d % per_tile, tile, 0.0)
        shift = (me % per_tile - d % per_tile + per_tile) % per_tile * cap
        mail[d] = pltpu.roll(tile, shift, 1)[:4]
    each(devices, lambda o: mail_copy(o).start())

    loads[4].wait()
    k_local = wave.shape[1]
    part = 1536 if k_local % 1536 == 0 else k_local
    found = None
    for first in range(0, k_local, part):
        w = wave[:, first : first + part]
        h, k, l = w[0:1], w[1:2], w[2:3]
        flip = l < 0
        s1 = jnp.where((h < 0) ^ flip, -1.0, 1.0)
        s2 = jnp.where((k < 0) ^ flip, -1.0, 1.0)
        h, k, l = jnp.abs(h), jnp.abs(k), jnp.abs(l)
        lone_k = (h == 0) & (k > 0)
        s1 = jnp.where(h > 0, s1, 0.0)
        s2 = jnp.where(k > 0, s2, 0.0)
        signs = (
            jnp.where(lone_k, 0.0, 1.0),
            jnp.where(lone_k, 1.0, s1 * s2),
            s1,
            jnp.where(lone_k, -s2, jnp.where(h > 0, s2, 0.0)),
        )
        of_l = l == iota((L_ROWS, part), 0) + 1
        left = jnp.concatenate([jnp.where(of_l, s, 0.0).astype(BF16) for s in signs])
        right = jnp.where(quad_of(h, k) == iota((QUADS, part), 0), 1.0, 0.0).astype(BF16)
        more = mm(left, right, NT)
        found = more if found is None else found + more
    lane_block = iota((L_ROWS, 128), 1) >> 5
    tail = jnp.concatenate([found[:, 128:QUADS]] * 4, axis=1)
    for t in range(W_TILES):
        merged = None
        for c in range(4):
            of_c = (found[:, :128] if t < 4 else tail)[L_ROWS * c : L_ROWS * (c + 1)]
            shift = 32 * (c - t) % 128
            if t < 4 and shift:
                of_c = pltpu.roll(of_c, shift, 1)
            merged = of_c if merged is None else jnp.where(lane_block == c, of_c, merged)
        for i in range(L_ROWS // 8):
            hist[t * (L_ROWS // 8) + i] = merged[8 * i : 8 * i + 8]
    hist_sib_copy().start()

    lanes = lambda part, first, n: table.at[:, pl.ds(part * both + first, n)]
    fill_plane(coords[0:1], coords[1:2], lanes(0, 0, slots), lanes(1, 0, slots))
    z = column(coords[2:3])
    acc[...] = sums_of(z * q, table[:, :slots], table[:, both : both + slots])
    hist_sib_copy().wait_recv()
    hist_chip[...] = hist[...] + hist_sib[...]
    each(ys, lambda o: hist_copy(o).start())

    def take(o, buf):
        fill_plane(got_ion[o, 0:1], got_ion[o, 1:2], buf.at[:, pl.ds(0, slots)], buf.at[:, pl.ds(slots, slots)])

    def add(o, buf):
        v = column(got_ion[o, 2:3], got_ion[o, 3:4])
        acc[...] += sums_of(v, buf[:, :slots], buf[:, slots:])

    if chips <= 16:
        for o in range(1, chips):
            ion_copy(o).wait_recv()
            take(o, (even, odd)[o % 2])
            if o > 1:
                add(o - 1, (even, odd)[(o - 1) % 2])
        add(chips - 1, (even, odd)[(chips - 1) % 2])
    else:

        def one(o):
            ion_copy(o).wait_recv()
            take(o, even)
            add(o, even)

        pl.loop(1, chips)(one)
    for i in range(2 * L_ROWS // 8):
        for t in range(W_TILES):
            sums[i * W_TILES + t] = acc[8 * i : 8 * i + 8, 128 * t : 128 * t + 128]
    sums_copy().start()

    each(devices, lambda o: mail_copy(o).wait_recv())
    got_mail[0] = mail[me]
    arrived = []
    for t in range(devices // per_tile):
        tile = jnp.zeros((4, 128), F32)
        for s in range(t * per_tile, (t + 1) * per_tile):
            db = lax.rem(blk - s // rows + blks, blks)
            dr = lax.rem(row - s % rows + rows, rows)
            tile = tile + got_mail[db * rows + dr]
        arrived.append(tile)
    came = jnp.concatenate(arrived, axis=1)
    came = jnp.concatenate([came, jnp.zeros_like(came)])
    loads[5].wait()
    index = recv_index[...].reshape(1, atoms)
    picks = jnp.where(index == iota((came.shape[1], atoms), 0), 1.0, 0.0).astype(BF16)
    ions = mm3(came, picks, NN)
    fill_plane(ions[0:1], ions[1:2], lanes(0, slots, atoms), lanes(1, slots, atoms))
    z = jnp.concatenate([z, column(ions[2:3])], axis=1)
    charge = jnp.concatenate([q, ions[3:4]], axis=1)

    each(ys, lambda o: hist_copy(o).wait_recv())
    times = hist_chip[...]
    for o in range(1, ys):
        times = times + got_hist[o]
    hf, kf, block, regular = lane_waves()
    l_col = (iota((L_ROWS, 1), 0) + 1).astype(F32)
    px, py, pz = TWO_PI * hf, TWO_PI * kf, TWO_PI * l_col / BOX_Z
    k2 = px * px + py * py + pz * pz
    weight = jnp.exp(-k2 / (4.0 * EWALD_BETA * EWALD_BETA)) / k2
    mix = []
    for t in range(W_TILES):
        at = slice(128 * t, 128 * t + 128)
        n = t * (L_ROWS // 8)
        m = jnp.concatenate([times[n + i] for i in range(L_ROWS // 8)]) * weight[:, at]
        rolled = [m] + [pltpu.roll(m, 32 * i, 1) for i in range(1, 4)]
        b = block[:, at]

        def spread(c):
            value = rolled[(3 - c) % 4]
            for n in range(3):
                value = jnp.where(b == n, rolled[(n - c) % 4], value)
            return value

        m0, m1, m2, m3 = (spread(c) for c in range(4))
        if 32 * (t + 1) > REGULAR:
            reg, is_odd = regular[:, at], (b & 1) == 1
            m0, m2 = (
                jnp.where(reg, m0, jnp.where(is_odd, m1, m0)),
                jnp.where(reg, m2, jnp.where(is_odd, m3, m2)),
            )
            m1, m3 = jnp.where(reg, m1, 0.0), jnp.where(reg, m3, 0.0)
        m1 = jnp.where(b < 2, -m1, m1)
        m2 = jnp.where((b == 0) | (b == 3), -m2, m2)
        m3 = jnp.where((b & 1) == 0, -m3, m3)
        mix.append((m0, m1, m2, m3))

    sums_copy().wait_recv()
    c_x, c_y = [], []
    c_all = []
    for t in range(W_TILES):
        at = slice(128 * t, 128 * t + 128)
        b = block[:, at]
        even_b = (b & 1) == 0
        total = jnp.concatenate(
            [sums[i * W_TILES + t] + from_sib[i * W_TILES + t] for i in range(2 * L_ROWS // 8)]
        )
        m0, m1, m2, m3 = mix[t]

        def partners(v):
            r1, r2, r3 = (pltpu.roll(v, 32 * i, 1) for i in range(1, 4))
            return jnp.where(even_b, r3, r1), r2, jnp.where(even_b, r1, r3)

        t1, t2, t3 = partners(total)
        re, im = slice(0, L_ROWS), slice(L_ROWS, 2 * L_ROWS)
        c = jnp.concatenate(
            [
                m0 * total[re] + m1 * t1[re] + m2 * t2[im] + m3 * t3[im],
                m0 * total[im] + m1 * t1[im] - m2 * t2[re] - m3 * t3[re],
            ]
        )
        _, c2, c3 = partners(c)
        h, k, reg = hf[:, at], kf[:, at], regular[:, at]
        c_all.append(c)
        c_x.append(c2 * jnp.where((b == 1) | (b == 2), -h, h))
        k_signed = jnp.where(even_b, k, -k)
        if 32 * (t + 1) > REGULAR:
            lone = jnp.where(b == 1, k, jnp.where(b == 3, -k, 0.0))
            c_y.append(c3 * jnp.where(reg, k_signed, 0.0) + c2 * jnp.where(reg, 0.0, lone))
        else:
            c_y.append(c3 * k_signed)
    ch, cl = split2(
        jnp.concatenate([jnp.concatenate(v, axis=1) for v in (c_all, c_x, c_y)])
    )
    n = ch.shape[0]
    x = mm(jnp.concatenate([ch, cl]), table[:, :both], NN)
    x = x[:n] + x[n:] + mm(ch, table[:, both:], NN)
    zc, zs = z[:L_ROWS], z[L_ROWS:]
    fz = jnp.sum(
        (x[L_ROWS : 2 * L_ROWS] * zc - x[:L_ROWS] * zs) * l_col, axis=0, keepdims=True
    )
    fx = jnp.sum(x[2 * L_ROWS : 4 * L_ROWS] * z, axis=0, keepdims=True)
    fy = jnp.sum(x[4 * L_ROWS :] * z, axis=0, keepdims=True)
    gain = (-scale * TWO_PI) * charge
    forces[...] = gain * jnp.concatenate([fx, fy, fz * (1.0 / BOX_Z)])

    each(chips, lambda o: ion_copy(o).wait_send())
    each(devices, lambda o: mail_copy(o).wait_send())
    hist_sib_copy().wait_send()
    each(ys, lambda o: hist_copy(o).wait_send())
    sums_copy().wait_send()


def deliver(counts, forces, slot_forces, atom_forces):
    slots = slot_forces.shape[1]
    live = iota((1, slots), 1) < jnp.broadcast_to(counts[...].reshape(1, 1), (1, slots))
    slot_forces[...] = jnp.where(live, forces[:, :slots], 0.0)
    atom_forces[...] = forces[:, slots:]


VMEM = pl.BlockSpec(memory_space=pltpu.VMEM)
ANY = pl.BlockSpec(memory_space=pl.ANY)


def body(coords, charges, counts, send_slot, recv_index, wave_ints):
    slots = charges.shape[0]
    atoms = recv_index.shape[0]
    blks, rows = lax.axis_size("blk"), lax.axis_size("row")
    devices = blks * rows
    chips = devices // 2
    cap = 2 * atoms // devices
    scale = FORCE_GAIN / math.sqrt(float(atoms * devices * blks * wave_ints.shape[1]))
    shape = jax.ShapeDtypeStruct
    args = (coords, charges, counts, send_slot, recv_index, wave_ints)
    dma = lambda n: [pltpu.SemaphoreType.DMA((n,))] * 2
    forces = pl.pallas_call(
        functools.partial(kernel, blks, rows, cap, scale),
        out_shape=shape((3, slots + atoms), F32),
        in_specs=[ANY] * 6,
        out_specs=VMEM,
        scratch_shapes=[pltpu.VMEM(a.shape, a.dtype) for a in args]
        + [
            pltpu.VMEM((WAVES, 2 * (slots + atoms)), BF16),
            pltpu.VMEM((WAVES, 2 * slots), BF16),
            pltpu.VMEM((WAVES, 2 * slots), BF16),
            pltpu.VMEM((4, slots), F32),
            pltpu.VMEM((chips, 4, slots), F32),
            pltpu.VMEM((devices, 4, 128), F32),
            pltpu.VMEM((devices, 4, 128), F32),
            pltpu.VMEM((H_TILES, 8, 128), F32),
            pltpu.VMEM((H_TILES, 8, 128), F32),
            pltpu.VMEM((H_TILES, 8, 128), F32),
            pltpu.VMEM((blks // 2, H_TILES, 8, 128), F32),
            pltpu.VMEM((2 * L_ROWS, WAVES), F32),
            pltpu.VMEM((T_TILES, 8, 128), F32),
            pltpu.VMEM((T_TILES, 8, 128), F32),
        ]
        + [pltpu.SemaphoreType.DMA((6,))]
        + dma(chips) + dma(devices) + dma(1) + dma(blks // 2) + dma(1),
        compiler_params=pltpu.CompilerParams(
            collective_id=0, has_side_effects=True, vmem_limit_bytes=56 * 2**20
        ),
    )(*args)
    return pl.pallas_call(
        deliver,
        out_shape=[shape((3, slots), F32), shape((3, atoms), F32)],
        in_specs=[VMEM] * 2,
        out_specs=[VMEM] * 2,
    )(counts, forces)


def solution(mesh):
    ions = P(("groups", "blk", "row"))
    return jax.shard_map(
        body,
        mesh=mesh,
        in_specs=(P(None, *ions), ions, ions, ions, ions, P(None, "blk")),
        out_specs=(P(None, *ions), P(None, *ions)),
        check_vma=False,
    )
```

```python
import functools
import math

import jax
import jax.numpy as jnp
import numpy as np
from jax import lax
from jax.experimental import pallas as pl
from jax.experimental.pallas import tpu as pltpu
from jax.sharding import PartitionSpec as P

EWALD_BETA = 30.0
BOX_Z = 3.0
FORCE_GAIN = 400.0
HMAX = 12
LMAX = 36
L_ROWS = 40
QUADS = 160
REGULAR = HMAX * HMAX
WAVES = 4 * QUADS
W_TILES = WAVES // 128
H_TILES = L_ROWS // 8 * W_TILES
T_TILES = 2 * H_TILES
F32 = jnp.float32
BF16 = jnp.bfloat16
NT = (((1,), (1,)), ((), ()))
NN = (((1,), (0,)), ((), ()))
TWO_PI = 2.0 * math.pi


def fit(f, terms):
    n = 64
    u = 0.125 + 0.125 * np.cos((2 * np.arange(n) + 1) * np.pi / (2 * n))
    c = np.polynomial.chebyshev.Chebyshev.fit(u, f(np.sqrt(u)), terms - 1, domain=[0.0, 0.25])
    return [float(v) for v in c.convert(kind=np.polynomial.Polynomial).coef]


SIN_C = fit(lambda r: np.sin(np.pi * r) / r, 5)
COS_C = fit(lambda r: np.cos(np.pi * r), 5)


def iota(shape, dim):
    return lax.broadcasted_iota(jnp.int32, shape, dim)


def horner(coefs, u):
    out = u * coefs[-1] + coefs[-2]
    for c in coefs[-3::-1]:
        out = out * u + c
    return out


def turns(mult, frac):
    t = mult * frac
    r = t - jnp.floor(t + 0.5)
    u = r * r
    s = r * horner(SIN_C, u)
    c = horner(COS_C, u)
    twice = s + s
    return 1.0 - twice * s, twice * c


def split2(x):
    hi = x.astype(BF16)
    return hi, (x - hi.astype(F32)).astype(BF16)


def split3(x):
    hi = x.astype(BF16)
    rest = x - hi.astype(F32)
    mid = rest.astype(BF16)
    return hi, mid, (rest - mid.astype(F32)).astype(BF16)


def mm(a, b, dims):
    return lax.dot_general(a, b, dims, preferred_element_type=F32)


def mm3(x, picks, dims):
    rows = x.shape[0]
    out = mm(jnp.concatenate(split3(x)), picks, dims)
    return out[:rows] + out[rows : 2 * rows] + out[2 * rows :]


def quad_of(h, k):
    even = jnp.where(k <= 8, 8 * h + k - 9, 83 + 4 * h + k)
    lone = jnp.where(h + k == 0, REGULAR + HMAX, REGULAR - 1 + h + k)
    return jnp.where((h > 0) & (k > 0), even, lone)


def lane_waves():
    lane = iota((1, WAVES), 1)
    block = (lane >> 5) & 3
    quad = ((lane >> 7) << 5) + (lane & 31)
    late = quad - 96
    h = jnp.where(quad < 96, (quad >> 3) + 1, (late >> 2) + 1)
    k = jnp.where(quad < 96, (quad & 7) + 1, (late & 3) + 9)
    lone = jnp.where(quad < REGULAR + HMAX, quad - (REGULAR - 1), 0)
    regular = quad < REGULAR
    odd = (block & 1) == 1
    h = jnp.where(regular, h, jnp.where(odd, 0, lone))
    k = jnp.where(regular, k, jnp.where(odd, lone, 0))
    return h.astype(F32), k.astype(F32), block, regular


def fill_plane(frac_x, frac_y, hi, lo):
    width = frac_x.shape[1]
    row = iota((16, 1), 0)
    mult = jnp.where(row < 12, row + 1, row - 3).astype(F32)
    cx, sx = turns(mult, frac_x)
    cy, sy = turns(mult, frac_y)
    low = iota((8, width), 0) < 4

    def two(v, i):
        a = jnp.broadcast_to(v[i : i + 1], (8, width))
        return jnp.where(low, a, jnp.broadcast_to(v[i + 1 : i + 2], (8, width)))

    def unit(u):
        if u < HMAX:
            a, b = cx[u : u + 1], sx[u : u + 1]
            c, d = cy[:8], sy[:8]
        elif u < 18:
            i = 2 * (u - HMAX)
            a, b = two(cx, i), two(sx, i)
            c, d = cy[8:], sy[8:]
        elif u == 18:
            return cx[:8], cy[:8], sx[:8], sy[:8]
        else:
            return jnp.where(low, cx[8:], 1.0), cy[8:], jnp.where(low, sx[8:], 0.0), sy[8:]
        return a * c, b * d, b * c, a * d

    for t in range(W_TILES):
        units = [unit(4 * t + i) for i in range(4)]
        for block in range(4):
            value = jnp.concatenate([v[block] for v in units])
            place = pl.ds(128 * t + 32 * block, 32)
            hi[place, :], lo[place, :] = split2(value)


def column(frac_z, gain=None):
    c, s = turns((iota((8, 1), 0) + 1).astype(F32), frac_z)
    c8, s8 = c[7:8], s[7:8]
    if gain is not None:
        c, s = c * gain, s * gain
    cs, ss = [c], [s]
    for _ in range(L_ROWS // 8 - 1):
        c, s = c * c8 - s * s8, s * c8 + c * s8
        cs.append(c)
        ss.append(s)
    return jnp.concatenate(cs + ss)


def sums_of(v, hi, lo):
    out = mm(v[...], hi, NT)
    return out[: 2 * L_ROWS] + out[2 * L_ROWS :] + mm(v[: 2 * L_ROWS], lo, NT)


def each(count, f):
    if count <= 16:
        for o in range(1, count):
            f(o)
    else:
        pl.loop(1, count)(f)


def kernel(
    blks, rows, cap, scale,
    coords_in, charges_in, counts_in, send_in, recv_in, wave_in,
    forces,
    coords, charges, counts, send_slot, recv_index, wave,
    table, even, odd, ion, got_ion, mail, got_mail,
    hist, hist_sib, hist_chip, got_hist, acc, sums, from_sib, coefs, zed, gain, found, even_v, odd_v,
    in_s, i_s, i_r, m_s, m_r, h_s, h_r, y_s, y_r, x_s, x_r,
):
    devices = blks * rows
    chips = devices // 2
    ys = blks // 2
    slots = coords.shape[1]
    atoms = recv_index.shape[0]
    both = slots + atoms
    blk, row = lax.axis_index("blk"), lax.axis_index("row")
    core = lax.rem(blk, 2)
    y = lax.div(blk, 2)
    me = blk * rows + row
    mesh_id = pl.DeviceIdType.MESH
    sibling = {"blk": blk + 1 - 2 * core, "row": row}

    loads = [
        pltpu.make_async_copy(src, dst, in_s.at[i])
        for i, (src, dst) in enumerate(
            (
                (coords_in, coords), (charges_in, charges), (counts_in, counts),
                (send_in, send_slot), (wave_in, wave), (recv_in, recv_index),
            )
        )
    ]
    for load in loads:
        load.start()

    blk_at = [lax.rem(blk + i, blks) for i in range(blks)]
    row_at = [lax.rem(row + i, rows) for i in range(rows)]

    def other(o):
        if isinstance(o, int):
            return {"blk": blk_at[o // rows], "row": row_at[o % rows]}
        return {"blk": lax.rem(blk + lax.div(o, rows), blks), "row": lax.rem(row + lax.rem(o, rows), rows)}

    def other_chip(o):
        if isinstance(o, int):
            return {"blk": blk_at[2 * (o // rows)], "row": row_at[o % rows]}
        return other(2 * rows * lax.div(o, rows) + lax.rem(o, rows))

    def copy(src, dst, s, r, o, dev):
        return pltpu.make_async_remote_copy(
            src_ref=src, dst_ref=dst, send_sem=s.at[o], recv_sem=r.at[o],
            device_id=dev, device_id_type=mesh_id,
        )

    def ion_copy(o):
        return copy(ion, got_ion.at[o], i_s, i_r, o, other_chip(o))

    def mail_copy(o):
        dev = other(o)
        return copy(mail.at[dev["blk"] * rows + dev["row"]], got_mail.at[o], m_s, m_r, o, dev)

    def hist_sib_copy():
        return copy(hist, hist_sib, h_s, h_r, 0, sibling)

    def hist_copy(o):
        return copy(hist_chip, got_hist.at[o], y_s, y_r, o, other_chip(o * rows))

    def sums_copy():
        return copy(sums, from_sib, x_s, x_r, 0, sibling)

    barrier = pltpu.get_barrier_semaphore()
    each(
        devices,
        lambda o: pl.semaphore_signal(
            barrier, inc=1, device_id=other(o), device_id_type=mesh_id
        ),
    )

    for load in loads[:3]:
        load.wait()
    live = iota((1, slots), 1) < jnp.broadcast_to(counts[...].reshape(1, 1), (1, slots))
    q = jnp.where(live, charges[...].reshape(1, slots), 0.0)
    ion[0:3] = coords[...]
    ion[3:4] = q
    pl.semaphore_wait(barrier, devices - 1)
    each(chips, lambda o: ion_copy(o).start())

    loads[3].wait()
    target = jnp.where(live, send_slot[...].reshape(1, slots), -1)
    spots = jnp.where(target == iota((devices * cap, slots), 0), 1.0, 0.0).astype(BF16)
    entries = jnp.concatenate([coords[...], q, jnp.zeros((4, slots), F32)])
    out = mm3(entries, spots, NT)
    per_tile = 128 // cap
    lane_part = iota((8, 128), 1) // cap
    for d in range(devices):
        tile = out[:, 128 * (d // per_tile) : 128 * (d // per_tile) + 128]
        tile = jnp.where(lane_part == d % per_tile, tile, 0.0)
        shift = (me % per_tile - d % per_tile + per_tile) % per_tile * cap
        mail[d] = pltpu.roll(tile, shift, 1)[:4]
    each(devices, lambda o: mail_copy(o).start())

    loads[4].wait()
    k_local = wave.shape[1]
    part = 1536 if k_local % 1536 == 0 else k_local
    found[...] = jnp.zeros_like(found)

    def count(i):
        w = wave[:, pl.ds(pl.multiple_of(i * part, 128), part)]
        h, k, l = w[0:1], w[1:2], w[2:3]
        flip = l < 0
        s1 = jnp.where((h < 0) ^ flip, -1.0, 1.0)
        s2 = jnp.where((k < 0) ^ flip, -1.0, 1.0)
        h, k, l = jnp.abs(h), jnp.abs(k), jnp.abs(l)
        lone_k = (h == 0) & (k > 0)
        s1 = jnp.where(h > 0, s1, 0.0)
        s2 = jnp.where(k > 0, s2, 0.0)
        signs = (
            jnp.where(lone_k, 0.0, 1.0),
            jnp.where(lone_k, 1.0, s1 * s2),
            s1,
            jnp.where(lone_k, -s2, jnp.where(h > 0, s2, 0.0)),
        )
        of_l = l == iota((L_ROWS, part), 0) + 1
        left = jnp.concatenate([jnp.where(of_l, s, 0.0).astype(BF16) for s in signs])
        right = jnp.where(quad_of(h, k) == iota((QUADS, part), 0), 1.0, 0.0).astype(BF16)
        half = part // 2
        found[...] += mm(left[:, :half], right[:, :half], NT) + mm(left[:, half:], right[:, half:], NT)

    pl.loop(0, k_local // part)(count)
    lane_block = iota((L_ROWS, 128), 1) >> 5
    tail = jnp.concatenate([found[:, 128:QUADS]] * 4, axis=1)
    for t in range(W_TILES):
        merged = None
        for c in range(4):
            of_c = (found[:, :128] if t < 4 else tail)[L_ROWS * c : L_ROWS * (c + 1)]
            shift = 32 * (c - t) % 128
            if t < 4 and shift:
                of_c = pltpu.roll(of_c, shift, 1)
            merged = of_c if merged is None else jnp.where(lane_block == c, of_c, merged)
        for i in range(L_ROWS // 8):
            hist[t * (L_ROWS // 8) + i] = merged[8 * i : 8 * i + 8]
    hist_sib_copy().start()

    lanes = lambda part, first, n: table.at[:, pl.ds(part * both + first, n)]
    fill_plane(coords[0:1], coords[1:2], lanes(0, 0, slots), lanes(1, 0, slots))
    z = column(coords[2:3])

    def put(v, value):
        v[: 2 * L_ROWS], v[2 * L_ROWS :] = split2(value)

    def take(o, buf, v):
        put(v, column(got_ion[o, 2:3], got_ion[o, 3:4]))
        fill_plane(got_ion[o, 0:1], got_ion[o, 1:2], buf.at[:, pl.ds(0, slots)], buf.at[:, pl.ds(slots, slots)])

    def add(buf, v):
        acc[...] += sums_of(v, buf[:, :slots], buf[:, slots:])

    put(even_v, z * q)
    hist_sib_copy().wait_recv()
    hist_chip[...] = hist[...] + hist_sib[...]
    each(ys, lambda o: hist_copy(o).start())
    ion_copy(1).wait_recv()
    acc[...] = sums_of(even_v, table[:, :slots], table[:, both : both + slots])
    take(1, odd, odd_v)

    def pair(i):
        o = 2 * i + 2
        ion_copy(o).wait_recv()
        add(odd, odd_v)
        take(o, even, even_v)
        ion_copy(o + 1).wait_recv()
        add(even, even_v)
        take(o + 1, odd, odd_v)

    pl.loop(0, chips // 2 - 1)(pair)
    add(odd, odd_v)
    for i in range(2 * L_ROWS // 8):
        for t in range(W_TILES):
            sums[i * W_TILES + t] = acc[8 * i : 8 * i + 8, 128 * t : 128 * t + 128]
    sums_copy().start()

    each(devices, lambda o: mail_copy(o).wait_recv())
    got_mail[0] = mail[me]
    arrived = []
    for t in range(devices // per_tile):
        tile = jnp.zeros((4, 128), F32)
        for s in range(t * per_tile, (t + 1) * per_tile):
            db = lax.rem(blk - s // rows + blks, blks)
            dr = lax.rem(row - s % rows + rows, rows)
            tile = tile + got_mail[db * rows + dr]
        arrived.append(tile)
    came = jnp.concatenate(arrived, axis=1)
    came = jnp.concatenate([came, jnp.zeros_like(came)])
    loads[5].wait()
    index = recv_index[...].reshape(1, atoms)
    picks = jnp.where(index == iota((came.shape[1], atoms), 0), 1.0, 0.0).astype(BF16)
    ions = mm3(came, picks, NN)
    fill_plane(ions[0:1], ions[1:2], lanes(0, slots, atoms), lanes(1, slots, atoms))
    zed[:, :slots] = z
    zed[:, slots:] = column(ions[2:3])
    gain[...] = (-scale * TWO_PI) * jnp.concatenate([q, ions[3:4]], axis=1)

    each(ys, lambda o: hist_copy(o).wait_recv())
    times = hist_chip[...]
    for o in range(1, ys):
        times = times + got_hist[o]
    hf, kf, block, regular = lane_waves()
    l_col = (iota((L_ROWS, 1), 0) + 1).astype(F32)
    px, py, pz = TWO_PI * hf, TWO_PI * kf, TWO_PI * l_col / BOX_Z
    k2 = px * px + py * py + pz * pz
    weight = jnp.exp(-k2 / (4.0 * EWALD_BETA * EWALD_BETA)) / k2
    mix = []
    for t in range(W_TILES):
        at = slice(128 * t, 128 * t + 128)
        n = t * (L_ROWS // 8)
        m = jnp.concatenate([times[n + i] for i in range(L_ROWS // 8)]) * weight[:, at]
        rolled = [m] + [pltpu.roll(m, 32 * i, 1) for i in range(1, 4)]
        b = block[:, at]

        def spread(c):
            value = rolled[(3 - c) % 4]
            for n in range(3):
                value = jnp.where(b == n, rolled[(n - c) % 4], value)
            return value

        m0, m1, m2, m3 = (spread(c) for c in range(4))
        if 32 * (t + 1) > REGULAR:
            reg, is_odd = regular[:, at], (b & 1) == 1
            m0, m2 = (
                jnp.where(reg, m0, jnp.where(is_odd, m1, m0)),
                jnp.where(reg, m2, jnp.where(is_odd, m3, m2)),
            )
            m1, m3 = jnp.where(reg, m1, 0.0), jnp.where(reg, m3, 0.0)
        m1 = jnp.where(b < 2, -m1, m1)
        m2 = jnp.where((b == 0) | (b == 3), -m2, m2)
        m3 = jnp.where((b & 1) == 0, -m3, m3)
        mix.append((m0, m1, m2, m3))

    sums_copy().wait_recv()
    c_x, c_y = [], []
    c_all = []
    for t in range(W_TILES):
        at = slice(128 * t, 128 * t + 128)
        b = block[:, at]
        even_b = (b & 1) == 0
        total = jnp.concatenate(
            [sums[i * W_TILES + t] + from_sib[i * W_TILES + t] for i in range(2 * L_ROWS // 8)]
        )
        m0, m1, m2, m3 = mix[t]

        def partners(v):
            r1, r2, r3 = (pltpu.roll(v, 32 * i, 1) for i in range(1, 4))
            return jnp.where(even_b, r3, r1), r2, jnp.where(even_b, r1, r3)

        t1, t2, t3 = partners(total)
        re, im = slice(0, L_ROWS), slice(L_ROWS, 2 * L_ROWS)
        c = jnp.concatenate(
            [
                m0 * total[re] + m1 * t1[re] + m2 * t2[im] + m3 * t3[im],
                m0 * total[im] + m1 * t1[im] - m2 * t2[re] - m3 * t3[re],
            ]
        )
        _, c2, c3 = partners(c)
        h, k, reg = hf[:, at], kf[:, at], regular[:, at]
        c_all.append(c)
        c_x.append(c2 * jnp.where((b == 1) | (b == 2), -h, h))
        k_signed = jnp.where(even_b, k, -k)
        if 32 * (t + 1) > REGULAR:
            lone = jnp.where(b == 1, k, jnp.where(b == 3, -k, 0.0))
            c_y.append(c3 * jnp.where(reg, k_signed, 0.0) + c2 * jnp.where(reg, 0.0, lone))
        else:
            c_y.append(c3 * k_signed)
    ch, cl = split2(
        jnp.concatenate([jnp.concatenate(v, axis=1) for v in (c_all, c_x, c_y)])
    )
    n = ch.shape[0]
    coefs[:n] = ch
    coefs[n:] = cl
    half = both // 2

    def pull(i):
        at = pl.ds(pl.multiple_of(i * half, 128), half)
        x = mm(coefs[...], table[:, at], NN)
        x = x[:n] + x[n:] + mm(coefs[:n], table[:, pl.ds(pl.multiple_of(both + i * half, 128), half)], NN)
        zc, zs = zed[:L_ROWS, at], zed[L_ROWS:, at]
        z = zed[:, at]
        fz = jnp.sum(
            (x[L_ROWS : 2 * L_ROWS] * zc - x[:L_ROWS] * zs) * l_col, axis=0, keepdims=True
        )
        fx = jnp.sum(x[2 * L_ROWS : 4 * L_ROWS] * z, axis=0, keepdims=True)
        fy = jnp.sum(x[4 * L_ROWS :] * z, axis=0, keepdims=True)
        forces[:, at] = gain[:, at] * jnp.concatenate([fx, fy, fz * (1.0 / BOX_Z)])

    pl.loop(0, 2)(pull)

    each(chips, lambda o: ion_copy(o).wait_send())
    each(devices, lambda o: mail_copy(o).wait_send())
    hist_sib_copy().wait_send()
    each(ys, lambda o: hist_copy(o).wait_send())
    sums_copy().wait_send()


def deliver(counts, forces, slot_forces, atom_forces):
    slots = slot_forces.shape[1]
    live = iota((1, slots), 1) < jnp.broadcast_to(counts[...].reshape(1, 1), (1, slots))
    slot_forces[...] = jnp.where(live, forces[:, :slots], 0.0)
    atom_forces[...] = forces[:, slots:]


VMEM = pl.BlockSpec(memory_space=pltpu.VMEM)
ANY = pl.BlockSpec(memory_space=pl.ANY)


def body(coords, charges, counts, send_slot, recv_index, wave_ints):
    slots = charges.shape[0]
    atoms = recv_index.shape[0]
    blks, rows = lax.axis_size("blk"), lax.axis_size("row")
    devices = blks * rows
    chips = devices // 2
    cap = 2 * atoms // devices
    scale = FORCE_GAIN / math.sqrt(float(atoms * devices * blks * wave_ints.shape[1]))
    shape = jax.ShapeDtypeStruct
    args = (coords, charges, counts, send_slot, recv_index, wave_ints)
    dma = lambda n: [pltpu.SemaphoreType.DMA((n,))] * 2
    forces = pl.pallas_call(
        functools.partial(kernel, blks, rows, cap, scale),
        out_shape=shape((3, slots + atoms), F32),
        in_specs=[ANY] * 6,
        out_specs=VMEM,
        scratch_shapes=[pltpu.VMEM(a.shape, a.dtype) for a in args]
        + [
            pltpu.VMEM((WAVES, 2 * (slots + atoms)), BF16),
            pltpu.VMEM((WAVES, 2 * slots), BF16),
            pltpu.VMEM((WAVES, 2 * slots), BF16),
            pltpu.VMEM((4, slots), F32),
            pltpu.VMEM((chips, 4, slots), F32),
            pltpu.VMEM((devices, 4, 128), F32),
            pltpu.VMEM((devices, 4, 128), F32),
            pltpu.VMEM((H_TILES, 8, 128), F32),
            pltpu.VMEM((H_TILES, 8, 128), F32),
            pltpu.VMEM((H_TILES, 8, 128), F32),
            pltpu.VMEM((blks // 2, H_TILES, 8, 128), F32),
            pltpu.VMEM((2 * L_ROWS, WAVES), F32),
            pltpu.VMEM((T_TILES, 8, 128), F32),
            pltpu.VMEM((T_TILES, 8, 128), F32),
            pltpu.VMEM((12 * L_ROWS, WAVES), BF16),
            pltpu.VMEM((2 * L_ROWS, slots + atoms), F32),
            pltpu.VMEM((1, slots + atoms), F32),
            pltpu.VMEM((4 * L_ROWS, QUADS), F32),
            pltpu.VMEM((4 * L_ROWS, slots), BF16),
            pltpu.VMEM((4 * L_ROWS, slots), BF16),
        ]
        + [pltpu.SemaphoreType.DMA((6,))]
        + dma(chips) + dma(devices) + dma(1) + dma(blks // 2) + dma(1),
        compiler_params=pltpu.CompilerParams(
            collective_id=0, has_side_effects=True, vmem_limit_bytes=56 * 2**20
        ),
    )(*args)
    return pl.pallas_call(
        deliver,
        out_shape=[shape((3, slots), F32), shape((3, atoms), F32)],
        in_specs=[VMEM] * 2,
        out_specs=[VMEM] * 2,
    )(counts, forces)


def solution(mesh):
    ions = P(("groups", "blk", "row"))
    return jax.shard_map(
        body,
        mesh=mesh,
        in_specs=(P(None, *ions), ions, ions, ions, ions, P(None, "blk")),
        out_specs=(P(None, *ions), P(None, *ions)),
        check_vma=False,
    )
```

```python
import functools
import math

import jax
import jax.numpy as jnp
import numpy as np
from jax import lax
from jax.experimental import pallas as pl
from jax.experimental.pallas import tpu as pltpu
from jax.sharding import PartitionSpec as P

EWALD_BETA = 30.0
BOX_Z = 3.0
FORCE_GAIN = 400.0
HMAX = 12
LMAX = 36
L_ROWS = 40
QUADS = 160
REGULAR = HMAX * HMAX
WAVES = 4 * QUADS
W_TILES = WAVES // 128
H_TILES = L_ROWS // 8 * W_TILES
T_TILES = 2 * H_TILES
F32 = jnp.float32
BF16 = jnp.bfloat16
NT = (((1,), (1,)), ((), ()))
NN = (((1,), (0,)), ((), ()))
TWO_PI = 2.0 * math.pi


def fit(f, terms):
    n = 64
    u = 0.125 + 0.125 * np.cos((2 * np.arange(n) + 1) * np.pi / (2 * n))
    c = np.polynomial.chebyshev.Chebyshev.fit(u, f(np.sqrt(u)), terms - 1, domain=[0.0, 0.25])
    return [float(v) for v in c.convert(kind=np.polynomial.Polynomial).coef]


SIN_C = fit(lambda r: np.sin(np.pi * r) / r, 5)
COS_C = fit(lambda r: np.cos(np.pi * r), 5)


def iota(shape, dim):
    return lax.broadcasted_iota(jnp.int32, shape, dim)


def horner(coefs, u):
    out = u * coefs[-1] + coefs[-2]
    for c in coefs[-3::-1]:
        out = out * u + c
    return out


def turns(mult, frac):
    t = mult * frac
    r = t - jnp.floor(t + 0.5)
    u = r * r
    s = r * horner(SIN_C, u)
    c = horner(COS_C, u)
    twice = s + s
    return 1.0 - twice * s, twice * c


def split2(x):
    hi = x.astype(BF16)
    return hi, (x - hi.astype(F32)).astype(BF16)


def split3(x):
    hi = x.astype(BF16)
    rest = x - hi.astype(F32)
    mid = rest.astype(BF16)
    return hi, mid, (rest - mid.astype(F32)).astype(BF16)


def mm(a, b, dims):
    return lax.dot_general(a, b, dims, preferred_element_type=F32)


def mm3(x, picks, dims):
    rows = x.shape[0]
    out = mm(jnp.concatenate(split3(x)), picks, dims)
    return out[:rows] + out[rows : 2 * rows] + out[2 * rows :]


def quad_of(h, k):
    even = jnp.where(k <= 8, 8 * h + k - 9, 83 + 4 * h + k)
    lone = jnp.where(h + k == 0, REGULAR + HMAX, REGULAR - 1 + h + k)
    return jnp.where((h > 0) & (k > 0), even, lone)


def lane_waves():
    lane = iota((1, WAVES), 1)
    block = (lane >> 5) & 3
    quad = ((lane >> 7) << 5) + (lane & 31)
    late = quad - 96
    h = jnp.where(quad < 96, (quad >> 3) + 1, (late >> 2) + 1)
    k = jnp.where(quad < 96, (quad & 7) + 1, (late & 3) + 9)
    lone = jnp.where(quad < REGULAR + HMAX, quad - (REGULAR - 1), 0)
    regular = quad < REGULAR
    odd = (block & 1) == 1
    h = jnp.where(regular, h, jnp.where(odd, 0, lone))
    k = jnp.where(regular, k, jnp.where(odd, lone, 0))
    return h.astype(F32), k.astype(F32), block, regular


def fill_plane(frac_x, frac_y, hi, lo):
    width = frac_x.shape[1]
    row = iota((16, 1), 0)
    mult = jnp.where(row < 12, row + 1, row - 3).astype(F32)
    cx, sx = turns(mult, frac_x)
    cy, sy = turns(mult, frac_y)
    low = iota((8, width), 0) < 4

    def two(v, i):
        a = jnp.broadcast_to(v[i : i + 1], (8, width))
        return jnp.where(low, a, jnp.broadcast_to(v[i + 1 : i + 2], (8, width)))

    def unit(u):
        if u < HMAX:
            a, b = cx[u : u + 1], sx[u : u + 1]
            c, d = cy[:8], sy[:8]
        elif u < 18:
            i = 2 * (u - HMAX)
            a, b = two(cx, i), two(sx, i)
            c, d = cy[8:], sy[8:]
        elif u == 18:
            return cx[:8], cy[:8], sx[:8], sy[:8]
        else:
            return jnp.where(low, cx[8:], 1.0), cy[8:], jnp.where(low, sx[8:], 0.0), sy[8:]
        return a * c, b * d, b * c, a * d

    for t in range(W_TILES):
        units = [unit(4 * t + i) for i in range(4)]
        for block in range(4):
            value = jnp.concatenate([v[block] for v in units])
            place = pl.ds(128 * t + 32 * block, 32)
            hi[place, :], lo[place, :] = split2(value)


def column(frac_z, gain=None):
    c, s = turns((iota((8, 1), 0) + 1).astype(F32), frac_z)
    c8, s8 = c[7:8], s[7:8]
    if gain is not None:
        c, s = c * gain, s * gain
    cs, ss = [c], [s]
    for _ in range(L_ROWS // 8 - 1):
        c, s = c * c8 - s * s8, s * c8 + c * s8
        cs.append(c)
        ss.append(s)
    return jnp.concatenate(cs + ss)


def sums_of(v, hi, lo):
    out = mm(v[...], hi, NT)
    return out[: 2 * L_ROWS] + out[2 * L_ROWS :] + mm(v[: 2 * L_ROWS], lo, NT)


def each(count, f):
    if count <= 16:
        for o in range(1, count):
            f(o)
    else:
        pl.loop(1, count)(f)


def kernel(
    blks, rows, cap, scale,
    coords_in, charges_in, counts_in, send_in, recv_in, wave_in,
    forces,
    coords, charges, counts, send_slot, recv_index, wave,
    table, even, odd, ion, got_ion, mail, got_mail,
    hist, hist_sib, hist_chip, got_hist, acc, sums, from_sib, zed, gain, found, even_v, odd_v,
    in_s, i_s, i_r, m_s, m_r, h_s, h_r, y_s, y_r, x_s, x_r,
):
    devices = blks * rows
    chips = devices // 2
    ys = blks // 2
    slots = coords.shape[1]
    atoms = recv_index.shape[0]
    both = slots + atoms
    blk, row = lax.axis_index("blk"), lax.axis_index("row")
    core = lax.rem(blk, 2)
    y = lax.div(blk, 2)
    me = blk * rows + row
    mesh_id = pl.DeviceIdType.MESH
    sibling = {"blk": blk + 1 - 2 * core, "row": row}

    loads = [
        pltpu.make_async_copy(src, dst, in_s.at[i])
        for i, (src, dst) in enumerate(
            (
                (coords_in, coords), (charges_in, charges), (counts_in, counts),
                (send_in, send_slot), (wave_in, wave), (recv_in, recv_index),
            )
        )
    ]
    for load in loads:
        load.start()

    blk_at = [lax.rem(blk + i, blks) for i in range(blks)]
    row_at = [lax.rem(row + i, rows) for i in range(rows)]

    def other(o):
        if isinstance(o, int):
            return {"blk": blk_at[o // rows], "row": row_at[o % rows]}
        return {"blk": lax.rem(blk + lax.div(o, rows), blks), "row": lax.rem(row + lax.rem(o, rows), rows)}

    def other_chip(o):
        if isinstance(o, int):
            return {"blk": blk_at[2 * (o // rows)], "row": row_at[o % rows]}
        return other(2 * rows * lax.div(o, rows) + lax.rem(o, rows))

    def copy(src, dst, s, r, o, dev):
        return pltpu.make_async_remote_copy(
            src_ref=src, dst_ref=dst, send_sem=s.at[o], recv_sem=r.at[o],
            device_id=dev, device_id_type=mesh_id,
        )

    def ion_copy(o):
        return copy(ion, got_ion.at[o], i_s, i_r, o, other_chip(o))

    def mail_copy(o):
        dev = other(o)
        return copy(mail.at[dev["blk"] * rows + dev["row"]], got_mail.at[o], m_s, m_r, o, dev)

    def hist_sib_copy():
        return copy(hist, hist_sib, h_s, h_r, 0, sibling)

    def hist_copy(o):
        return copy(hist_chip, got_hist.at[o], y_s, y_r, o, other_chip(o * rows))

    def sums_copy():
        return copy(sums, from_sib, x_s, x_r, 0, sibling)

    barrier = pltpu.get_barrier_semaphore()
    each(
        devices,
        lambda o: pl.semaphore_signal(
            barrier, inc=1, device_id=other(o), device_id_type=mesh_id
        ),
    )

    for load in loads[:3]:
        load.wait()
    live = iota((1, slots), 1) < jnp.broadcast_to(counts[...].reshape(1, 1), (1, slots))
    q = jnp.where(live, charges[...].reshape(1, slots), 0.0)
    ion[0:3] = coords[...]
    ion[3:4] = q
    pl.semaphore_wait(barrier, devices - 1)
    each(chips, lambda o: ion_copy(o).start())

    loads[3].wait()
    target = jnp.where(live, send_slot[...].reshape(1, slots), -1)
    spots = jnp.where(target == iota((devices * cap, slots), 0), 1.0, 0.0).astype(BF16)
    entries = jnp.concatenate([coords[...], q, jnp.zeros((4, slots), F32)])
    out = mm3(entries, spots, NT)
    per_tile = 128 // cap
    lane_part = iota((8, 128), 1) // cap
    for d in range(devices):
        tile = out[:, 128 * (d // per_tile) : 128 * (d // per_tile) + 128]
        tile = jnp.where(lane_part == d % per_tile, tile, 0.0)
        shift = (me % per_tile - d % per_tile + per_tile) % per_tile * cap
        mail[d] = pltpu.roll(tile, shift, 1)[:4]
    each(devices, lambda o: mail_copy(o).start())

    loads[4].wait()
    k_local = wave.shape[1]
    part = 1536 if k_local % 1536 == 0 else k_local
    found[...] = jnp.zeros_like(found)

    def count(i):
        w = wave[:, pl.ds(pl.multiple_of(i * part, 128), part)]
        h, k, l = w[0:1], w[1:2], w[2:3]
        flip = l < 0
        s1 = jnp.where((h < 0) ^ flip, -1.0, 1.0)
        s2 = jnp.where((k < 0) ^ flip, -1.0, 1.0)
        h, k, l = jnp.abs(h), jnp.abs(k), jnp.abs(l)
        lone_k = (h == 0) & (k > 0)
        s1 = jnp.where(h > 0, s1, 0.0)
        s2 = jnp.where(k > 0, s2, 0.0)
        signs = (
            jnp.where(lone_k, 0.0, 1.0),
            jnp.where(lone_k, 1.0, s1 * s2),
            s1,
            jnp.where(lone_k, -s2, jnp.where(h > 0, s2, 0.0)),
        )
        of_l = l == iota((L_ROWS, part), 0) + 1
        left = jnp.concatenate([jnp.where(of_l, s, 0.0).astype(BF16) for s in signs])
        right = jnp.where(quad_of(h, k) == iota((QUADS, part), 0), 1.0, 0.0).astype(BF16)
        half = part // 2
        found[...] += mm(left[:, :half], right[:, :half], NT) + mm(left[:, half:], right[:, half:], NT)

    pl.loop(0, k_local // part)(count)
    lane_block = iota((L_ROWS, 128), 1) >> 5
    tail = jnp.concatenate([found[:, 128:QUADS]] * 4, axis=1)
    for t in range(W_TILES):
        merged = None
        for c in range(4):
            of_c = (found[:, :128] if t < 4 else tail)[L_ROWS * c : L_ROWS * (c + 1)]
            shift = 32 * (c - t) % 128
            if t < 4 and shift:
                of_c = pltpu.roll(of_c, shift, 1)
            merged = of_c if merged is None else jnp.where(lane_block == c, of_c, merged)
        for i in range(L_ROWS // 8):
            hist[t * (L_ROWS // 8) + i] = merged[8 * i : 8 * i + 8]
    hist_sib_copy().start()

    lanes = lambda part, first, n: table.at[pl.ds(part * WAVES, WAVES), pl.ds(first, n)]
    fill_plane(coords[0:1], coords[1:2], lanes(0, 0, slots), lanes(1, 0, slots))
    z = column(coords[2:3])

    def put(v, value):
        v[: 2 * L_ROWS], v[2 * L_ROWS :] = split2(value)

    def take(o, buf, v):
        put(v, column(got_ion[o, 2:3], got_ion[o, 3:4]))
        fill_plane(got_ion[o, 0:1], got_ion[o, 1:2], buf.at[:, pl.ds(0, slots)], buf.at[:, pl.ds(slots, slots)])

    def add(buf, v):
        acc[...] += sums_of(v, buf[:, :slots], buf[:, slots:])

    put(even_v, z * q)
    ion_copy(1).wait_recv()
    acc[...] = sums_of(even_v, table[:WAVES, :slots], table[WAVES:, :slots])
    take(1, odd, odd_v)

    hist_sib_copy().wait_recv()
    hist_chip[...] = hist[...] + hist_sib[...]
    each(ys, lambda o: hist_copy(o).start())

    def pair(i):
        o = 2 * i + 2
        ion_copy(o).wait_recv()
        add(odd, odd_v)
        take(o, even, even_v)
        ion_copy(o + 1).wait_recv()
        add(even, even_v)
        take(o + 1, odd, odd_v)

    pl.loop(0, chips // 2 - 1)(pair)
    add(odd, odd_v)
    for i in range(2 * L_ROWS // 8):
        for t in range(W_TILES):
            sums[i * W_TILES + t] = acc[8 * i : 8 * i + 8, 128 * t : 128 * t + 128]
    sums_copy().start()

    each(devices, lambda o: mail_copy(o).wait_recv())
    got_mail[0] = mail[me]
    arrived = []
    for t in range(devices // per_tile):
        tile = jnp.zeros((4, 128), F32)
        for s in range(t * per_tile, (t + 1) * per_tile):
            db = lax.rem(blk - s // rows + blks, blks)
            dr = lax.rem(row - s % rows + rows, rows)
            tile = tile + got_mail[db * rows + dr]
        arrived.append(tile)
    came = jnp.concatenate(arrived, axis=1)
    came = jnp.concatenate([came, jnp.zeros_like(came)])
    loads[5].wait()
    index = recv_index[...].reshape(1, atoms)
    picks = jnp.where(index == iota((came.shape[1], atoms), 0), 1.0, 0.0).astype(BF16)
    ions = mm3(came, picks, NN)
    fill_plane(ions[0:1], ions[1:2], lanes(0, slots, atoms), lanes(1, slots, atoms))
    zed[:, :slots] = z
    zed[:, slots:] = column(ions[2:3])
    gain[...] = (-scale * TWO_PI) * jnp.concatenate([q, ions[3:4]], axis=1)

    each(ys, lambda o: hist_copy(o).wait_recv())
    times = hist_chip[...]
    for o in range(1, ys):
        times = times + got_hist[o]
    hf, kf, block, regular = lane_waves()
    l_col = (iota((L_ROWS, 1), 0) + 1).astype(F32)
    px, py, pz = TWO_PI * hf, TWO_PI * kf, TWO_PI * l_col / BOX_Z
    k2 = px * px + py * py + pz * pz
    weight = jnp.exp(-k2 / (4.0 * EWALD_BETA * EWALD_BETA)) / k2
    mix = []
    for t in range(W_TILES):
        at = slice(128 * t, 128 * t + 128)
        n = t * (L_ROWS // 8)
        m = jnp.concatenate([times[n + i] for i in range(L_ROWS // 8)]) * weight[:, at]
        rolled = [m] + [pltpu.roll(m, 32 * i, 1) for i in range(1, 4)]
        b = block[:, at]

        def spread(c):
            value = rolled[(3 - c) % 4]
            for n in range(3):
                value = jnp.where(b == n, rolled[(n - c) % 4], value)
            return value

        m0, m1, m2, m3 = (spread(c) for c in range(4))
        if 32 * (t + 1) > REGULAR:
            reg, is_odd = regular[:, at], (b & 1) == 1
            m0, m2 = (
                jnp.where(reg, m0, jnp.where(is_odd, m1, m0)),
                jnp.where(reg, m2, jnp.where(is_odd, m3, m2)),
            )
            m1, m3 = jnp.where(reg, m1, 0.0), jnp.where(reg, m3, 0.0)
        m1 = jnp.where(b < 2, -m1, m1)
        m2 = jnp.where((b == 0) | (b == 3), -m2, m2)
        m3 = jnp.where((b & 1) == 0, -m3, m3)
        mix.append((m0, m1, m2, m3))

    sums_copy().wait_recv()
    c_x, c_y = [], []
    c_all = []
    for t in range(W_TILES):
        at = slice(128 * t, 128 * t + 128)
        b = block[:, at]
        even_b = (b & 1) == 0
        total = jnp.concatenate(
            [sums[i * W_TILES + t] + from_sib[i * W_TILES + t] for i in range(2 * L_ROWS // 8)]
        )
        m0, m1, m2, m3 = mix[t]

        def partners(v):
            r1, r2, r3 = (pltpu.roll(v, 32 * i, 1) for i in range(1, 4))
            return jnp.where(even_b, r3, r1), r2, jnp.where(even_b, r1, r3)

        t1, t2, t3 = partners(total)
        re, im = slice(0, L_ROWS), slice(L_ROWS, 2 * L_ROWS)
        c = jnp.concatenate(
            [
                m0 * total[re] + m1 * t1[re] + m2 * t2[im] + m3 * t3[im],
                m0 * total[im] + m1 * t1[im] - m2 * t2[re] - m3 * t3[re],
            ]
        )
        _, c2, c3 = partners(c)
        h, k, reg = hf[:, at], kf[:, at], regular[:, at]
        c_all.append(c)
        c_x.append(c2 * jnp.where((b == 1) | (b == 2), -h, h))
        k_signed = jnp.where(even_b, k, -k)
        if 32 * (t + 1) > REGULAR:
            lone = jnp.where(b == 1, k, jnp.where(b == 3, -k, 0.0))
            c_y.append(c3 * jnp.where(reg, k_signed, 0.0) + c2 * jnp.where(reg, 0.0, lone))
        else:
            c_y.append(c3 * k_signed)
    ch, cl = split2(
        jnp.concatenate([jnp.concatenate(v, axis=1) for v in (c_all, c_x, c_y)])
    )
    x = mm(jnp.concatenate([ch, ch], axis=1), table[...], NN)
    x = x + mm(cl, table[:WAVES], NN)
    z = zed[...]
    zc, zs = z[:L_ROWS], z[L_ROWS:]
    fz = jnp.sum(
        (x[L_ROWS : 2 * L_ROWS] * zc - x[:L_ROWS] * zs) * l_col, axis=0, keepdims=True
    )
    fx = jnp.sum(x[2 * L_ROWS : 4 * L_ROWS] * z, axis=0, keepdims=True)
    fy = jnp.sum(x[4 * L_ROWS :] * z, axis=0, keepdims=True)
    forces[...] = gain[...] * jnp.concatenate([fx, fy, fz * (1.0 / BOX_Z)])

    each(chips, lambda o: ion_copy(o).wait_send())
    each(devices, lambda o: mail_copy(o).wait_send())
    hist_sib_copy().wait_send()
    each(ys, lambda o: hist_copy(o).wait_send())
    sums_copy().wait_send()


def deliver(counts, forces, slot_forces, atom_forces):
    slots = slot_forces.shape[1]
    live = iota((1, slots), 1) < jnp.broadcast_to(counts[...].reshape(1, 1), (1, slots))
    slot_forces[...] = jnp.where(live, forces[:, :slots], 0.0)
    atom_forces[...] = forces[:, slots:]


VMEM = pl.BlockSpec(memory_space=pltpu.VMEM)
ANY = pl.BlockSpec(memory_space=pl.ANY)


def body(coords, charges, counts, send_slot, recv_index, wave_ints):
    slots = charges.shape[0]
    atoms = recv_index.shape[0]
    blks, rows = lax.axis_size("blk"), lax.axis_size("row")
    devices = blks * rows
    chips = devices // 2
    cap = 2 * atoms // devices
    scale = FORCE_GAIN / math.sqrt(float(atoms * devices * blks * wave_ints.shape[1]))
    shape = jax.ShapeDtypeStruct
    args = (coords, charges, counts, send_slot, recv_index, wave_ints)
    dma = lambda n: [pltpu.SemaphoreType.DMA((n,))] * 2
    forces = pl.pallas_call(
        functools.partial(kernel, blks, rows, cap, scale),
        out_shape=shape((3, slots + atoms), F32),
        in_specs=[ANY] * 6,
        out_specs=VMEM,
        scratch_shapes=[pltpu.VMEM(a.shape, a.dtype) for a in args]
        + [
            pltpu.VMEM((2 * WAVES, slots + atoms), BF16),
            pltpu.VMEM((WAVES, 2 * slots), BF16),
            pltpu.VMEM((WAVES, 2 * slots), BF16),
            pltpu.VMEM((4, slots), F32),
            pltpu.VMEM((chips, 4, slots), F32),
            pltpu.VMEM((devices, 4, 128), F32),
            pltpu.VMEM((devices, 4, 128), F32),
            pltpu.VMEM((H_TILES, 8, 128), F32),
            pltpu.VMEM((H_TILES, 8, 128), F32),
            pltpu.VMEM((H_TILES, 8, 128), F32),
            pltpu.VMEM((blks // 2, H_TILES, 8, 128), F32),
            pltpu.VMEM((2 * L_ROWS, WAVES), F32),
            pltpu.VMEM((T_TILES, 8, 128), F32),
            pltpu.VMEM((T_TILES, 8, 128), F32),
            pltpu.VMEM((2 * L_ROWS, slots + atoms), F32),
            pltpu.VMEM((1, slots + atoms), F32),
            pltpu.VMEM((4 * L_ROWS, QUADS), F32),
            pltpu.VMEM((4 * L_ROWS, slots), BF16),
            pltpu.VMEM((4 * L_ROWS, slots), BF16),
        ]
        + [pltpu.SemaphoreType.DMA((6,))]
        + dma(chips) + dma(devices) + dma(1) + dma(blks // 2) + dma(1),
        compiler_params=pltpu.CompilerParams(
            collective_id=0, has_side_effects=True, vmem_limit_bytes=56 * 2**20
        ),
    )(*args)
    return pl.pallas_call(
        deliver,
        out_shape=[shape((3, slots), F32), shape((3, atoms), F32)],
        in_specs=[VMEM] * 2,
        out_specs=[VMEM] * 2,
    )(counts, forces)


def solution(mesh):
    ions = P(("groups", "blk", "row"))
    return jax.shard_map(
        body,
        mesh=mesh,
        in_specs=(P(None, *ions), ions, ions, ions, ions, P(None, "blk")),
        out_specs=(P(None, *ions), P(None, *ions)),
        check_vma=False,
    )
```

```python
import functools
import math

import jax
import jax.numpy as jnp
import numpy as np
from jax import lax
from jax.experimental import pallas as pl
from jax.experimental.pallas import tpu as pltpu
from jax.sharding import PartitionSpec as P

EWALD_BETA = 30.0
BOX_Z = 3.0
FORCE_GAIN = 400.0
HMAX = 12
LMAX = 36
L_ROWS = 40
QUADS = 160
REGULAR = HMAX * HMAX
WAVES = 4 * QUADS
W_TILES = WAVES // 128
H_TILES = L_ROWS // 8 * W_TILES
T_TILES = 2 * H_TILES
F32 = jnp.float32
BF16 = jnp.bfloat16
NT = (((1,), (1,)), ((), ()))
NN = (((1,), (0,)), ((), ()))
TWO_PI = 2.0 * math.pi


def fit(f, terms):
    n = 64
    u = 0.125 + 0.125 * np.cos((2 * np.arange(n) + 1) * np.pi / (2 * n))
    c = np.polynomial.chebyshev.Chebyshev.fit(u, f(np.sqrt(u)), terms - 1, domain=[0.0, 0.25])
    return [float(v) for v in c.convert(kind=np.polynomial.Polynomial).coef]


SIN_C = fit(lambda r: np.sin(np.pi * r) / r, 5)
COS_C = fit(lambda r: np.cos(np.pi * r), 5)


def iota(shape, dim):
    return lax.broadcasted_iota(jnp.int32, shape, dim)


def horner(coefs, u):
    out = u * coefs[-1] + coefs[-2]
    for c in coefs[-3::-1]:
        out = out * u + c
    return out


def turns(mult, frac):
    t = mult * frac
    r = t - jnp.floor(t + 0.5)
    u = r * r
    s = r * horner(SIN_C, u)
    c = horner(COS_C, u)
    twice = s + s
    return 1.0 - twice * s, twice * c


def split2(x):
    hi = x.astype(BF16)
    return hi, (x - hi.astype(F32)).astype(BF16)


def split3(x):
    hi = x.astype(BF16)
    rest = x - hi.astype(F32)
    mid = rest.astype(BF16)
    return hi, mid, (rest - mid.astype(F32)).astype(BF16)


def mm(a, b, dims):
    return lax.dot_general(a, b, dims, preferred_element_type=F32)


def mm3(x, picks, dims):
    rows = x.shape[0]
    out = mm(jnp.concatenate(split3(x)), picks, dims)
    return out[:rows] + out[rows : 2 * rows] + out[2 * rows :]


def quad_of(h, k):
    even = jnp.where(k <= 8, 8 * h + k - 9, 83 + 4 * h + k)
    lone = jnp.where(h + k == 0, REGULAR + HMAX, REGULAR - 1 + h + k)
    return jnp.where((h > 0) & (k > 0), even, lone)


def lane_waves():
    lane = iota((1, WAVES), 1)
    block = (lane >> 5) & 3
    quad = ((lane >> 7) << 5) + (lane & 31)
    late = quad - 96
    h = jnp.where(quad < 96, (quad >> 3) + 1, (late >> 2) + 1)
    k = jnp.where(quad < 96, (quad & 7) + 1, (late & 3) + 9)
    lone = jnp.where(quad < REGULAR + HMAX, quad - (REGULAR - 1), 0)
    regular = quad < REGULAR
    odd = (block & 1) == 1
    h = jnp.where(regular, h, jnp.where(odd, 0, lone))
    k = jnp.where(regular, k, jnp.where(odd, lone, 0))
    return h.astype(F32), k.astype(F32), block, regular


def fill_plane(frac_x, frac_y, hi, lo):
    width = frac_x.shape[1]
    row = iota((16, 1), 0)
    mult = jnp.where(row < 12, row + 1, row - 3).astype(F32)
    cx, sx = turns(mult, frac_x)
    cy, sy = turns(mult, frac_y)
    low = iota((8, width), 0) < 4

    def two(v, i):
        a = jnp.broadcast_to(v[i : i + 1], (8, width))
        return jnp.where(low, a, jnp.broadcast_to(v[i + 1 : i + 2], (8, width)))

    def unit(u):
        if u < HMAX:
            a, b = cx[u : u + 1], sx[u : u + 1]
            c, d = cy[:8], sy[:8]
        elif u < 18:
            i = 2 * (u - HMAX)
            a, b = two(cx, i), two(sx, i)
            c, d = cy[8:], sy[8:]
        elif u == 18:
            return cx[:8], cy[:8], sx[:8], sy[:8]
        else:
            return jnp.where(low, cx[8:], 1.0), cy[8:], jnp.where(low, sx[8:], 0.0), sy[8:]
        return a * c, b * d, b * c, a * d

    for t in range(W_TILES):
        units = [unit(4 * t + i) for i in range(4)]
        for block in range(4):
            value = jnp.concatenate([v[block] for v in units])
            place = pl.ds(128 * t + 32 * block, 32)
            hi[place, :], lo[place, :] = split2(value)


def column(frac_z, gain=None):
    c, s = turns((iota((8, 1), 0) + 1).astype(F32), frac_z)
    c8, s8 = c[7:8], s[7:8]
    if gain is not None:
        c, s = c * gain, s * gain
    cs, ss = [c], [s]
    for _ in range(L_ROWS // 8 - 1):
        c, s = c * c8 - s * s8, s * c8 + c * s8
        cs.append(c)
        ss.append(s)
    return jnp.concatenate(cs + ss)


def sums_of(v, hi, lo):
    out = mm(v[...], hi, NT)
    return out[: 2 * L_ROWS] + out[2 * L_ROWS :] + mm(v[: 2 * L_ROWS], lo, NT)


def each(count, f):
    if count <= 16:
        for o in range(1, count):
            f(o)
    else:
        pl.loop(1, count)(f)


def kernel(
    blks, rows, cap, scale,
    coords_in, charges_in, counts_in, send_in, recv_in, wave_in,
    slot_forces, atom_forces,
    coords, charges, counts, send_slot, recv_index, wave,
    table, even, odd, ion, got_ion, mail, got_mail,
    hist, hist_sib, hist_chip, got_hist, acc, sums, from_sib, zed, gain, found, even_v, odd_v,
    in_s, i_s, i_r, m_s, m_r, h_s, h_r, y_s, y_r, x_s, x_r,
):
    devices = blks * rows
    chips = devices // 2
    ys = blks // 2
    slots = coords.shape[1]
    atoms = recv_index.shape[0]
    both = slots + atoms
    blk, row = lax.axis_index("blk"), lax.axis_index("row")
    core = lax.rem(blk, 2)
    y = lax.div(blk, 2)
    me = blk * rows + row
    mesh_id = pl.DeviceIdType.MESH
    sibling = {"blk": blk + 1 - 2 * core, "row": row}

    loads = [
        pltpu.make_async_copy(src, dst, in_s.at[i])
        for i, (src, dst) in enumerate(
            (
                (coords_in, coords), (charges_in, charges), (counts_in, counts),
                (send_in, send_slot), (wave_in, wave), (recv_in, recv_index),
            )
        )
    ]
    for load in loads:
        load.start()

    blk_at = [lax.rem(blk + i, blks) for i in range(blks)]
    row_at = [lax.rem(row + i, rows) for i in range(rows)]

    def other(o):
        if isinstance(o, int):
            return {"blk": blk_at[o // rows], "row": row_at[o % rows]}
        return {"blk": lax.rem(blk + lax.div(o, rows), blks), "row": lax.rem(row + lax.rem(o, rows), rows)}

    def other_chip(o):
        if isinstance(o, int):
            return {"blk": blk_at[2 * (o % ys)], "row": row_at[o // ys]}
        return {"blk": lax.rem(blk + 2 * lax.rem(o, ys), blks), "row": lax.rem(row + lax.div(o, ys), rows)}

    def copy(src, dst, s, r, o, dev):
        return pltpu.make_async_remote_copy(
            src_ref=src, dst_ref=dst, send_sem=s.at[o], recv_sem=r.at[o],
            device_id=dev, device_id_type=mesh_id,
        )

    def ion_copy(o):
        return copy(ion, got_ion.at[o], i_s, i_r, o, other_chip(o))

    def mail_copy(o):
        dev = other(o)
        return copy(mail.at[dev["blk"] * rows + dev["row"]], got_mail.at[o], m_s, m_r, o, dev)

    def hist_sib_copy():
        return copy(hist, hist_sib, h_s, h_r, 0, sibling)

    def hist_copy(o):
        return copy(hist_chip, got_hist.at[o], y_s, y_r, o, other_chip(o))

    def sums_copy():
        return copy(sums, from_sib, x_s, x_r, 0, sibling)

    barrier = pltpu.get_barrier_semaphore()
    each(
        devices,
        lambda o: pl.semaphore_signal(
            barrier, inc=1, device_id=other(o), device_id_type=mesh_id
        ),
    )

    for load in loads[:3]:
        load.wait()
    live = iota((1, slots), 1) < jnp.broadcast_to(counts[...].reshape(1, 1), (1, slots))
    q = jnp.where(live, charges[...].reshape(1, slots), 0.0)
    ion[0:3] = coords[...]
    ion[3:4] = q
    pl.semaphore_wait(barrier, devices - 1)
    each(chips, lambda o: ion_copy(o).start())

    loads[3].wait()
    per_tile = 128 // cap
    target = jnp.where(live, send_slot[...].reshape(1, slots), -cap)
    dest = lax.shift_right_arithmetic(target, cap.bit_length() - 1)
    lane = (target & (cap - 1)) + lax.rem(me, per_tile) * cap
    spots = jnp.where(lane == iota((128, slots), 0), 1.0, 0.0).astype(BF16)
    quad = jnp.concatenate([coords[...], q] * 2)
    terms = [term.astype(F32) for term in split3(quad)]
    half = lax.shift_right_logical(iota((8, slots), 0), 2)
    places = [dest == half + d for d in range(0, devices, 2)]
    rows_of = [
        jnp.where(at, term, 0.0).astype(BF16) for term in terms for at in places
    ]
    out = mm(jnp.concatenate(rows_of), spots, NT)
    n = 4 * devices
    out = out[:n] + out[n : 2 * n] + out[2 * n :]
    for d in range(devices):
        mail[d] = out[4 * d : 4 * d + 4]
    each(devices, lambda o: mail_copy(o).start())

    loads[4].wait()
    k_local = wave.shape[1]
    part = 1536 if k_local % 1536 == 0 else k_local
    found[...] = jnp.zeros_like(found)

    def count(i):
        w = wave[:, pl.ds(pl.multiple_of(i * part, 128), part)]
        h, k, l = w[0:1], w[1:2], w[2:3]
        flip = l < 0
        s1 = jnp.where((h < 0) ^ flip, -1.0, 1.0)
        s2 = jnp.where((k < 0) ^ flip, -1.0, 1.0)
        h, k, l = jnp.abs(h), jnp.abs(k), jnp.abs(l)
        lone_k = (h == 0) & (k > 0)
        s1 = jnp.where(h > 0, s1, 0.0)
        s2 = jnp.where(k > 0, s2, 0.0)
        signs = (
            jnp.where(lone_k, 0.0, 1.0),
            jnp.where(lone_k, 1.0, s1 * s2),
            s1,
            jnp.where(lone_k, -s2, jnp.where(h > 0, s2, 0.0)),
        )
        of_l = l == iota((L_ROWS, part), 0) + 1
        left = jnp.concatenate([jnp.where(of_l, s, 0.0).astype(BF16) for s in signs])
        right = jnp.where(quad_of(h, k) == iota((QUADS, part), 0), 1.0, 0.0).astype(BF16)
        half = part // 2
        found[...] += mm(left[:, :half], right[:, :half], NT) + mm(left[:, half:], right[:, half:], NT)

    pl.loop(0, k_local // part)(count)
    lane_block = iota((L_ROWS, 128), 1) >> 5
    tail = jnp.concatenate([found[:, 128:QUADS]] * 4, axis=1)
    for t in range(W_TILES):
        merged = None
        for c in range(4):
            of_c = (found[:, :128] if t < 4 else tail)[L_ROWS * c : L_ROWS * (c + 1)]
            shift = 32 * (c - t) % 128
            if t < 4 and shift:
                of_c = pltpu.roll(of_c, shift, 1)
            merged = of_c if merged is None else jnp.where(lane_block == c, of_c, merged)
        for i in range(L_ROWS // 8):
            hist[t * (L_ROWS // 8) + i] = merged[8 * i : 8 * i + 8]
    hist_sib_copy().start()

    lanes = lambda part, first, n: table.at[pl.ds(part * WAVES, WAVES), pl.ds(first, n)]
    fill_plane(coords[0:1], coords[1:2], lanes(0, 0, slots), lanes(1, 0, slots))
    z = column(coords[2:3])

    def put(v, value):
        v[: 2 * L_ROWS], v[2 * L_ROWS :] = split2(value)

    def take(o, buf, v):
        put(v, column(got_ion[o, 2:3], got_ion[o, 3:4]))
        fill_plane(got_ion[o, 0:1], got_ion[o, 1:2], buf.at[:, pl.ds(0, slots)], buf.at[:, pl.ds(slots, slots)])

    def add(buf, v):
        acc[...] += sums_of(v, buf[:, :slots], buf[:, slots:])

    put(even_v, z * q)
    ion_copy(1).wait_recv()
    acc[...] = sums_of(even_v, table[:WAVES, :slots], table[WAVES:, :slots])
    take(1, odd, odd_v)

    hist_sib_copy().wait_recv()
    hist_chip[...] = hist[...] + hist_sib[...]
    each(ys, lambda o: hist_copy(o).start())

    def pair(i):
        o = 2 * i + 2
        ion_copy(o).wait_recv()
        ion_copy(o + 1).wait_recv()
        add(odd, odd_v)
        take(o, even, even_v)
        add(even, even_v)
        take(o + 1, odd, odd_v)

    pl.loop(0, chips // 2 - 1)(pair)
    add(odd, odd_v)
    for i in range(2 * L_ROWS // 8):
        for t in range(W_TILES):
            sums[i * W_TILES + t] = acc[8 * i : 8 * i + 8, 128 * t : 128 * t + 128]
    sums_copy().start()

    each(devices, lambda o: mail_copy(o).wait_recv())
    got_mail[0] = mail[me]
    arrived = []
    for s in range(devices):
        db = lax.rem(blk - s // rows + blks, blks)
        dr = lax.rem(row - s % rows + rows, rows)
        arrived.append(got_mail[db * rows + dr])
    loads[5].wait()
    index = recv_index[...].reshape(1, atoms)
    rank = index & (cap - 1)
    source = lax.shift_right_logical(index, cap.bit_length() - 1)
    picks = jnp.where(rank == (iota((128, atoms), 0) & (cap - 1)), 1.0, 0.0).astype(BF16)
    came = mm3(jnp.concatenate(arrived), picks, NN)
    half = lax.shift_right_logical(iota((8, atoms), 0), 2)
    ions = jnp.zeros((8, atoms), F32)
    for s in range(0, devices, 2):
        ions = ions + jnp.where(source == half + s, came[4 * s : 4 * s + 8], 0.0)
    ions = ions[:4] + ions[4:]
    fill_plane(ions[0:1], ions[1:2], lanes(0, slots, atoms), lanes(1, slots, atoms))
    zed[:, :slots] = z
    zed[:, slots:] = column(ions[2:3])
    gain[...] = (-scale * TWO_PI) * jnp.concatenate([q, ions[3:4]], axis=1)

    each(ys, lambda o: hist_copy(o).wait_recv())
    times = hist_chip[...]
    for o in range(1, ys):
        times = times + got_hist[o]
    hf, kf, block, regular = lane_waves()
    l_col = (iota((L_ROWS, 1), 0) + 1).astype(F32)
    px, py, pz = TWO_PI * hf, TWO_PI * kf, TWO_PI * l_col / BOX_Z
    k2 = px * px + py * py + pz * pz
    weight = jnp.exp(-k2 / (4.0 * EWALD_BETA * EWALD_BETA)) / k2
    mix = []
    for t in range(W_TILES):
        at = slice(128 * t, 128 * t + 128)
        n = t * (L_ROWS // 8)
        m = jnp.concatenate([times[n + i] for i in range(L_ROWS // 8)]) * weight[:, at]
        rolled = [m] + [pltpu.roll(m, 32 * i, 1) for i in range(1, 4)]
        b = block[:, at]

        def spread(c):
            value = rolled[(3 - c) % 4]
            for n in range(3):
                value = jnp.where(b == n, rolled[(n - c) % 4], value)
            return value

        m0, m1, m2, m3 = (spread(c) for c in range(4))
        if 32 * (t + 1) > REGULAR:
            reg, is_odd = regular[:, at], (b & 1) == 1
            m0, m2 = (
                jnp.where(reg, m0, jnp.where(is_odd, m1, m0)),
                jnp.where(reg, m2, jnp.where(is_odd, m3, m2)),
            )
            m1, m3 = jnp.where(reg, m1, 0.0), jnp.where(reg, m3, 0.0)
        m1 = jnp.where(b < 2, -m1, m1)
        m2 = jnp.where((b == 0) | (b == 3), -m2, m2)
        m3 = jnp.where((b & 1) == 0, -m3, m3)
        mix.append((m0, m1, m2, m3))

    sums_copy().wait_recv()
    c_x, c_y = [], []
    c_all = []
    for t in range(W_TILES):
        at = slice(128 * t, 128 * t + 128)
        b = block[:, at]
        even_b = (b & 1) == 0
        total = jnp.concatenate(
            [sums[i * W_TILES + t] + from_sib[i * W_TILES + t] for i in range(2 * L_ROWS // 8)]
        )
        m0, m1, m2, m3 = mix[t]

        def partners(v):
            r1, r2, r3 = (pltpu.roll(v, 32 * i, 1) for i in range(1, 4))
            return jnp.where(even_b, r3, r1), r2, jnp.where(even_b, r1, r3)

        t1, t2, t3 = partners(total)
        re, im = slice(0, L_ROWS), slice(L_ROWS, 2 * L_ROWS)
        c = jnp.concatenate(
            [
                m0 * total[re] + m1 * t1[re] + m2 * t2[im] + m3 * t3[im],
                m0 * total[im] + m1 * t1[im] - m2 * t2[re] - m3 * t3[re],
            ]
        )
        _, c2, c3 = partners(c)
        h, k, reg = hf[:, at], kf[:, at], regular[:, at]
        c_all.append(c)
        c_x.append(c2 * jnp.where((b == 1) | (b == 2), -h, h))
        k_signed = jnp.where(even_b, k, -k)
        if 32 * (t + 1) > REGULAR:
            lone = jnp.where(b == 1, k, jnp.where(b == 3, -k, 0.0))
            c_y.append(c3 * jnp.where(reg, k_signed, 0.0) + c2 * jnp.where(reg, 0.0, lone))
        else:
            c_y.append(c3 * k_signed)
    ch, cl = split2(
        jnp.concatenate([jnp.concatenate(v, axis=1) for v in (c_all, c_x, c_y)])
    )
    x = mm(jnp.concatenate([ch, ch], axis=1), table[...], NN)
    x = x + mm(cl, table[:WAVES], NN)
    z = zed[...]
    zc, zs = z[:L_ROWS], z[L_ROWS:]
    fz = jnp.sum(
        (x[L_ROWS : 2 * L_ROWS] * zc - x[:L_ROWS] * zs) * l_col, axis=0, keepdims=True
    )
    fx = jnp.sum(x[2 * L_ROWS : 4 * L_ROWS] * z, axis=0, keepdims=True)
    fy = jnp.sum(x[4 * L_ROWS :] * z, axis=0, keepdims=True)
    force = gain[...] * jnp.concatenate([fx, fy, fz * (1.0 / BOX_Z)])
    slot_forces[...] = jnp.where(live, force[:, :slots], 0.0)
    atom_forces[...] = force[:, slots:]

    each(chips, lambda o: ion_copy(o).wait_send())
    each(devices, lambda o: mail_copy(o).wait_send())
    hist_sib_copy().wait_send()
    each(ys, lambda o: hist_copy(o).wait_send())
    sums_copy().wait_send()


def deliver(slot_in, atom_in, slot_forces, atom_forces, sem):
    copies = [
        pltpu.make_async_copy(slot_in, slot_forces, sem.at[0]),
        pltpu.make_async_copy(atom_in, atom_forces, sem.at[1]),
    ]
    for copy in copies:
        copy.start()
    for copy in copies:
        copy.wait()


VMEM = pl.BlockSpec(memory_space=pltpu.VMEM)
HBM = pl.BlockSpec(memory_space=pltpu.HBM)
ANY = pl.BlockSpec(memory_space=pl.ANY)


def body(coords, charges, counts, send_slot, recv_index, wave_ints):
    slots = charges.shape[0]
    atoms = recv_index.shape[0]
    blks, rows = lax.axis_size("blk"), lax.axis_size("row")
    devices = blks * rows
    chips = devices // 2
    cap = 2 * atoms // devices
    scale = FORCE_GAIN / math.sqrt(float(atoms * devices * blks * wave_ints.shape[1]))
    shape = jax.ShapeDtypeStruct
    args = (coords, charges, counts, send_slot, recv_index, wave_ints)
    dma = lambda n: [pltpu.SemaphoreType.DMA((n,))] * 2
    slot_forces, atom_forces = pl.pallas_call(
        functools.partial(kernel, blks, rows, cap, scale),
        out_shape=[pltpu.VMEM((3, slots), F32), pltpu.VMEM((3, atoms), F32)],
        in_specs=[HBM] * 6,
        out_specs=[VMEM] * 2,
        scratch_shapes=[pltpu.VMEM(a.shape, a.dtype) for a in args]
        + [
            pltpu.VMEM((2 * WAVES, slots + atoms), BF16),
            pltpu.VMEM((WAVES, 2 * slots), BF16),
            pltpu.VMEM((WAVES, 2 * slots), BF16),
            pltpu.VMEM((4, slots), F32),
            pltpu.VMEM((chips, 4, slots), F32),
            pltpu.VMEM((devices, 4, 128), F32),
            pltpu.VMEM((devices, 4, 128), F32),
            pltpu.VMEM((H_TILES, 8, 128), F32),
            pltpu.VMEM((H_TILES, 8, 128), F32),
            pltpu.VMEM((H_TILES, 8, 128), F32),
            pltpu.VMEM((blks // 2, H_TILES, 8, 128), F32),
            pltpu.VMEM((2 * L_ROWS, WAVES), F32),
            pltpu.VMEM((T_TILES, 8, 128), F32),
            pltpu.VMEM((T_TILES, 8, 128), F32),
            pltpu.VMEM((2 * L_ROWS, slots + atoms), F32),
            pltpu.VMEM((1, slots + atoms), F32),
            pltpu.VMEM((4 * L_ROWS, QUADS), F32),
            pltpu.VMEM((4 * L_ROWS, slots), BF16),
            pltpu.VMEM((4 * L_ROWS, slots), BF16),
        ]
        + [pltpu.SemaphoreType.DMA((6,))]
        + dma(chips) + dma(devices) + dma(1) + dma(blks // 2) + dma(1),
        compiler_params=pltpu.CompilerParams(
            collective_id=0, has_side_effects=True, vmem_limit_bytes=56 * 2**20
        ),
    )(*args)
    return slot_forces, atom_forces


def solution(mesh):
    ions = P(("groups", "blk", "row"))
    return jax.shard_map(
        body,
        mesh=mesh,
        in_specs=(P(None, *ions), ions, ions, ions, ions, P(None, "blk")),
        out_specs=(P(None, *ions), P(None, *ions)),
        check_vma=False,
    )
```

```python
import functools
import math

import jax
import jax.numpy as jnp
import numpy as np
from jax import lax
from jax.experimental import pallas as pl
from jax.experimental.pallas import tpu as pltpu
from jax.sharding import PartitionSpec as P

EWALD_BETA = 30.0
BOX_Z = 3.0
FORCE_GAIN = 400.0
HMAX = 12
LMAX = 36
L_ROWS = 40
QUADS = 160
REGULAR = HMAX * HMAX
WAVES = 4 * QUADS
W_TILES = WAVES // 128
H_TILES = L_ROWS // 8 * W_TILES
T_TILES = 2 * H_TILES
F32 = jnp.float32
BF16 = jnp.bfloat16
NT = (((1,), (1,)), ((), ()))
NN = (((1,), (0,)), ((), ()))
TWO_PI = 2.0 * math.pi


def fit(f, terms):
    n = 64
    u = 0.125 + 0.125 * np.cos((2 * np.arange(n) + 1) * np.pi / (2 * n))
    c = np.polynomial.chebyshev.Chebyshev.fit(u, f(np.sqrt(u)), terms - 1, domain=[0.0, 0.25])
    return [float(v) for v in c.convert(kind=np.polynomial.Polynomial).coef]


SIN_C = fit(lambda r: np.sin(np.pi * r) / r, 5)
COS_C = fit(lambda r: np.cos(np.pi * r), 5)


def iota(shape, dim):
    return lax.broadcasted_iota(jnp.int32, shape, dim)


def horner(coefs, u):
    out = u * coefs[-1] + coefs[-2]
    for c in coefs[-3::-1]:
        out = out * u + c
    return out


def turns(mult, frac):
    t = mult * frac
    r = t - jnp.floor(t + 0.5)
    u = r * r
    s = r * horner(SIN_C, u)
    c = horner(COS_C, u)
    twice = s + s
    return 1.0 - twice * s, twice * c


def split2(x):
    hi = x.astype(BF16)
    return hi, (x - hi.astype(F32)).astype(BF16)


def split3(x):
    hi = x.astype(BF16)
    rest = x - hi.astype(F32)
    mid = rest.astype(BF16)
    return hi, mid, (rest - mid.astype(F32)).astype(BF16)


def mm(a, b, dims):
    return lax.dot_general(a, b, dims, preferred_element_type=F32)


def mm3(x, picks, dims):
    rows = x.shape[0]
    out = mm(jnp.concatenate(split3(x)), picks, dims)
    return out[:rows] + out[rows : 2 * rows] + out[2 * rows :]


def quad_of(h, k):
    even = jnp.where(k <= 8, 8 * h + k - 9, 83 + 4 * h + k)
    lone = jnp.where(h + k == 0, REGULAR + HMAX, REGULAR - 1 + h + k)
    return jnp.where((h > 0) & (k > 0), even, lone)


def lane_waves():
    lane = iota((1, WAVES), 1)
    block = (lane >> 5) & 3
    quad = ((lane >> 7) << 5) + (lane & 31)
    late = quad - 96
    h = jnp.where(quad < 96, (quad >> 3) + 1, (late >> 2) + 1)
    k = jnp.where(quad < 96, (quad & 7) + 1, (late & 3) + 9)
    lone = jnp.where(quad < REGULAR + HMAX, quad - (REGULAR - 1), 0)
    regular = quad < REGULAR
    odd = (block & 1) == 1
    h = jnp.where(regular, h, jnp.where(odd, 0, lone))
    k = jnp.where(regular, k, jnp.where(odd, lone, 0))
    return h.astype(F32), k.astype(F32), block, regular


def fill_plane(frac_x, frac_y, hi, lo):
    width = frac_x.shape[1]
    row = iota((16, 1), 0)
    mult = jnp.where(row < 12, row + 1, row - 3).astype(F32)
    cx, sx = turns(mult, frac_x)
    cy, sy = turns(mult, frac_y)
    low = iota((8, width), 0) < 4

    def two(v, i):
        a = jnp.broadcast_to(v[i : i + 1], (8, width))
        return jnp.where(low, a, jnp.broadcast_to(v[i + 1 : i + 2], (8, width)))

    def unit(u):
        if u < HMAX:
            a, b = cx[u : u + 1], sx[u : u + 1]
            c, d = cy[:8], sy[:8]
        elif u < 18:
            i = 2 * (u - HMAX)
            a, b = two(cx, i), two(sx, i)
            c, d = cy[8:], sy[8:]
        elif u == 18:
            return cx[:8], cy[:8], sx[:8], sy[:8]
        else:
            return jnp.where(low, cx[8:], 1.0), cy[8:], jnp.where(low, sx[8:], 0.0), sy[8:]
        return a * c, b * d, b * c, a * d

    for t in range(W_TILES):
        units = [unit(4 * t + i) for i in range(4)]
        for block in range(4):
            value = jnp.concatenate([v[block] for v in units])
            place = pl.ds(128 * t + 32 * block, 32)
            hi[place, :], lo[place, :] = split2(value)


def column(frac_z, gain=None):
    c, s = turns((iota((8, 1), 0) + 1).astype(F32), frac_z)
    c8, s8 = c[7:8], s[7:8]
    if gain is not None:
        c, s = c * gain, s * gain
    cs, ss = [c], [s]
    for _ in range(L_ROWS // 8 - 1):
        c, s = c * c8 - s * s8, s * c8 + c * s8
        cs.append(c)
        ss.append(s)
    return jnp.concatenate(cs + ss)


def sums_of(v, hi, lo):
    out = mm(v[...], hi, NT)
    return out[: 2 * L_ROWS] + out[2 * L_ROWS :] + mm(v[: 2 * L_ROWS], lo, NT)


def each(count, f):
    if count <= 16:
        for o in range(1, count):
            f(o)
    else:
        pl.loop(1, count)(f)


def kernel(
    blks, rows, cap, scale,
    coords_in, charges_in, counts_in, send_in, recv_in, wave_in,
    slot_forces, atom_forces,
    coords, charges, counts, send_slot, recv_index, wave,
    table, even, odd, ion, got_ion, mail, got_mail,
    hist, hist_sib, hist_chip, got_hist, acc, sums, from_sib, zed, gain, found, even_v, odd_v,
    in_s, i_s, i_r, m_s, m_r, h_s, h_r, y_s, y_r, x_s, x_r,
):
    devices = blks * rows
    chips = devices // 2
    ys = blks // 2
    slots = coords.shape[1]
    atoms = recv_index.shape[0]
    both = slots + atoms
    blk, row = lax.axis_index("blk"), lax.axis_index("row")
    core = lax.rem(blk, 2)
    y = lax.div(blk, 2)
    me = blk * rows + row
    mesh_id = pl.DeviceIdType.MESH
    sibling = {"blk": blk + 1 - 2 * core, "row": row}

    loads = [
        pltpu.make_async_copy(src, dst, in_s.at[i])
        for i, (src, dst) in enumerate(
            (
                (coords_in, coords), (charges_in, charges), (counts_in, counts),
                (send_in, send_slot), (wave_in, wave), (recv_in, recv_index),
            )
        )
    ]
    for load in loads:
        load.start()

    blk_at = [lax.rem(blk + i, blks) for i in range(blks)]
    row_at = [lax.rem(row + i, rows) for i in range(rows)]

    def other(o):
        if isinstance(o, int):
            return {"blk": blk_at[o // rows], "row": row_at[o % rows]}
        return {"blk": lax.rem(blk + lax.div(o, rows), blks), "row": lax.rem(row + lax.rem(o, rows), rows)}

    def other_chip(o):
        if isinstance(o, int):
            return {"blk": blk_at[2 * (o % ys)], "row": row_at[o // ys]}
        return {"blk": lax.rem(blk + 2 * lax.rem(o, ys), blks), "row": lax.rem(row + lax.div(o, ys), rows)}

    def copy(src, dst, s, r, o, dev):
        return pltpu.make_async_remote_copy(
            src_ref=src, dst_ref=dst, send_sem=s.at[o], recv_sem=r.at[o],
            device_id=dev, device_id_type=mesh_id,
        )

    def ion_copy(o):
        return copy(ion, got_ion.at[o], i_s, i_r, o, other_chip(o))

    def mail_copy(o):
        dev = other(o)
        return copy(mail.at[dev["blk"] * rows + dev["row"]], got_mail.at[o], m_s, m_r, o, dev)

    def hist_sib_copy():
        return copy(hist, hist_sib, h_s, h_r, 0, sibling)

    def hist_copy(o):
        return copy(hist_chip, got_hist.at[o], y_s, y_r, o, other_chip(o))

    def sums_copy():
        return copy(sums, from_sib, x_s, x_r, 0, sibling)

    barrier = pltpu.get_barrier_semaphore()
    each(
        devices,
        lambda o: pl.semaphore_signal(
            barrier, inc=1, device_id=other(o), device_id_type=mesh_id
        ),
    )

    for load in loads[:3]:
        load.wait()
    live = iota((1, slots), 1) < jnp.broadcast_to(counts[...].reshape(1, 1), (1, slots))
    q = jnp.where(live, charges[...].reshape(1, slots), 0.0)
    ion[0:3] = coords[...]
    ion[3:4] = q
    pl.semaphore_wait(barrier, devices - 1)
    each(chips, lambda o: ion_copy(o).start())

    loads[3].wait()
    per_tile = 128 // cap
    target = jnp.where(live, send_slot[...].reshape(1, slots), -cap)
    dest = lax.shift_right_arithmetic(target, cap.bit_length() - 1)
    lane = (target & (cap - 1)) + lax.rem(me, per_tile) * cap
    spots = jnp.where(lane == iota((128, slots), 0), 1.0, 0.0).astype(BF16)
    quad = jnp.concatenate([coords[...], q] * 2)
    terms = [term.astype(F32) for term in split3(quad)]
    half = lax.shift_right_logical(iota((8, slots), 0), 2)
    places = [dest == half + d for d in range(0, devices, 2)]
    rows_of = [
        jnp.where(at, term, 0.0).astype(BF16) for term in terms for at in places
    ]
    out = mm(jnp.concatenate(rows_of), spots, NT)
    n = 4 * devices
    out = out[:n] + out[n : 2 * n] + out[2 * n :]
    for d in range(devices):
        mail[d] = out[4 * d : 4 * d + 4]
    each(devices, lambda o: mail_copy(o).start())

    loads[4].wait()
    k_local = wave.shape[1]
    part = 1536 if k_local % 1536 == 0 else k_local
    found[...] = jnp.zeros_like(found)

    def count(i):
        w = wave[:, pl.ds(pl.multiple_of(i * part, 128), part)]
        h, k, l = w[0:1], w[1:2], w[2:3]
        flip = l < 0
        s1 = jnp.where((h < 0) ^ flip, -1.0, 1.0)
        s2 = jnp.where((k < 0) ^ flip, -1.0, 1.0)
        h, k, l = jnp.abs(h), jnp.abs(k), jnp.abs(l)
        lone_k = (h == 0) & (k > 0)
        s1 = jnp.where(h > 0, s1, 0.0)
        s2 = jnp.where(k > 0, s2, 0.0)
        signs = (
            jnp.where(lone_k, 0.0, 1.0),
            jnp.where(lone_k, 1.0, s1 * s2),
            s1,
            jnp.where(lone_k, -s2, jnp.where(h > 0, s2, 0.0)),
        )
        of_l = l == iota((L_ROWS, part), 0) + 1
        left = jnp.concatenate([jnp.where(of_l, s, 0.0).astype(BF16) for s in signs])
        right = jnp.where(quad_of(h, k) == iota((QUADS, part), 0), 1.0, 0.0).astype(BF16)
        half = part // 2
        found[...] += mm(left[:, :half], right[:, :half], NT) + mm(left[:, half:], right[:, half:], NT)

    pl.loop(0, k_local // part)(count)
    lane_block = iota((L_ROWS, 128), 1) >> 5
    tail = jnp.concatenate([found[:, 128:QUADS]] * 4, axis=1)
    for t in range(W_TILES):
        merged = None
        for c in range(4):
            of_c = (found[:, :128] if t < 4 else tail)[L_ROWS * c : L_ROWS * (c + 1)]
            shift = 32 * (c - t) % 128
            if t < 4 and shift:
                of_c = pltpu.roll(of_c, shift, 1)
            merged = of_c if merged is None else jnp.where(lane_block == c, of_c, merged)
        for i in range(L_ROWS // 8):
            hist[t * (L_ROWS // 8) + i] = merged[8 * i : 8 * i + 8]
    hist_sib_copy().start()

    lanes = lambda part, first, n: table.at[pl.ds(part * WAVES, WAVES), pl.ds(first, n)]
    fill_plane(coords[0:1], coords[1:2], lanes(0, 0, slots), lanes(1, 0, slots))
    z = column(coords[2:3])

    def put(v, value):
        v[: 2 * L_ROWS], v[2 * L_ROWS :] = split2(value)

    def take(o, buf, v):
        put(v, column(got_ion[o, 2:3], got_ion[o, 3:4]))
        fill_plane(got_ion[o, 0:1], got_ion[o, 1:2], buf.at[:, pl.ds(0, slots)], buf.at[:, pl.ds(slots, slots)])

    def add(buf, v):
        acc[...] += sums_of(v, buf[:, :slots], buf[:, slots:])

    put(even_v, z * q)
    ion_copy(1).wait_recv()
    acc[...] = sums_of(even_v, table[:WAVES, :slots], table[WAVES:, :slots])
    take(1, odd, odd_v)

    hist_sib_copy().wait_recv()
    hist_chip[...] = hist[...] + hist_sib[...]
    each(ys, lambda o: hist_copy(o).start())

    def pair(i):
        o = 2 * i + 2
        ion_copy(o).wait_recv()
        ion_copy(o + 1).wait_recv()
        add(odd, odd_v)
        take(o, even, even_v)
        add(even, even_v)
        take(o + 1, odd, odd_v)

    if chips <= 8:

        def rest(_):
            for o in range(2, chips):
                ion_copy(o).wait_recv()
            for o in range(2, chips, 2):
                add(odd, odd_v)
                take(o, even, even_v)
                add(even, even_v)
                take(o + 1, odd, odd_v)
            add(odd, odd_v)

        pl.loop(0, 1 + lax.div(blk, blks))(rest)
    else:
        pl.loop(0, chips // 2 - 1)(pair)
        add(odd, odd_v)
    for i in range(2 * L_ROWS // 8):
        for t in range(W_TILES):
            sums[i * W_TILES + t] = acc[8 * i : 8 * i + 8, 128 * t : 128 * t + 128]
    sums_copy().start()

    each(devices, lambda o: mail_copy(o).wait_recv())
    got_mail[0] = mail[me]
    arrived = []
    for s in range(devices):
        db = lax.rem(blk - s // rows + blks, blks)
        dr = lax.rem(row - s % rows + rows, rows)
        arrived.append(got_mail[db * rows + dr])
    loads[5].wait()
    index = recv_index[...].reshape(1, atoms)
    rank = index & (cap - 1)
    source = lax.shift_right_logical(index, cap.bit_length() - 1)
    picks = jnp.where(rank == (iota((128, atoms), 0) & (cap - 1)), 1.0, 0.0).astype(BF16)
    came = mm3(jnp.concatenate(arrived), picks, NN)
    half = lax.shift_right_logical(iota((8, atoms), 0), 2)
    ions = jnp.zeros((8, atoms), F32)
    for s in range(0, devices, 2):
        ions = ions + jnp.where(source == half + s, came[4 * s : 4 * s + 8], 0.0)
    ions = ions[:4] + ions[4:]
    fill_plane(ions[0:1], ions[1:2], lanes(0, slots, atoms), lanes(1, slots, atoms))
    zed[:, :slots] = z
    zed[:, slots:] = column(ions[2:3])
    gain[...] = (-scale * TWO_PI) * jnp.concatenate([q, ions[3:4]], axis=1)

    each(ys, lambda o: hist_copy(o).wait_recv())
    times = hist_chip[...]
    for o in range(1, ys):
        times = times + got_hist[o]
    hf, kf, block, regular = lane_waves()
    l_col = (iota((L_ROWS, 1), 0) + 1).astype(F32)
    px, py, pz = TWO_PI * hf, TWO_PI * kf, TWO_PI * l_col / BOX_Z
    k2 = px * px + py * py + pz * pz
    weight = jnp.exp(-k2 / (4.0 * EWALD_BETA * EWALD_BETA)) / k2
    mix = []
    for t in range(W_TILES):
        at = slice(128 * t, 128 * t + 128)
        n = t * (L_ROWS // 8)
        m = jnp.concatenate([times[n + i] for i in range(L_ROWS // 8)]) * weight[:, at]
        rolled = [m] + [pltpu.roll(m, 32 * i, 1) for i in range(1, 4)]
        b = block[:, at]

        def spread(c):
            value = rolled[(3 - c) % 4]
            for n in range(3):
                value = jnp.where(b == n, rolled[(n - c) % 4], value)
            return value

        m0, m1, m2, m3 = (spread(c) for c in range(4))
        if 32 * (t + 1) > REGULAR:
            reg, is_odd = regular[:, at], (b & 1) == 1
            m0, m2 = (
                jnp.where(reg, m0, jnp.where(is_odd, m1, m0)),
                jnp.where(reg, m2, jnp.where(is_odd, m3, m2)),
            )
            m1, m3 = jnp.where(reg, m1, 0.0), jnp.where(reg, m3, 0.0)
        m1 = jnp.where(b < 2, -m1, m1)
        m2 = jnp.where((b == 0) | (b == 3), -m2, m2)
        m3 = jnp.where((b & 1) == 0, -m3, m3)
        mix.append((m0, m1, m2, m3))

    sums_copy().wait_recv()
    c_x, c_y = [], []
    c_all = []
    for t in range(W_TILES):
        at = slice(128 * t, 128 * t + 128)
        b = block[:, at]
        even_b = (b & 1) == 0
        total = jnp.concatenate(
            [sums[i * W_TILES + t] + from_sib[i * W_TILES + t] for i in range(2 * L_ROWS // 8)]
        )
        m0, m1, m2, m3 = mix[t]

        def partners(v):
            r1, r2, r3 = (pltpu.roll(v, 32 * i, 1) for i in range(1, 4))
            return jnp.where(even_b, r3, r1), r2, jnp.where(even_b, r1, r3)

        t1, t2, t3 = partners(total)
        re, im = slice(0, L_ROWS), slice(L_ROWS, 2 * L_ROWS)
        c = jnp.concatenate(
            [
                m0 * total[re] + m1 * t1[re] + m2 * t2[im] + m3 * t3[im],
                m0 * total[im] + m1 * t1[im] - m2 * t2[re] - m3 * t3[re],
            ]
        )
        _, c2, c3 = partners(c)
        h, k, reg = hf[:, at], kf[:, at], regular[:, at]
        c_all.append(c)
        c_x.append(c2 * jnp.where((b == 1) | (b == 2), -h, h))
        k_signed = jnp.where(even_b, k, -k)
        if 32 * (t + 1) > REGULAR:
            lone = jnp.where(b == 1, k, jnp.where(b == 3, -k, 0.0))
            c_y.append(c3 * jnp.where(reg, k_signed, 0.0) + c2 * jnp.where(reg, 0.0, lone))
        else:
            c_y.append(c3 * k_signed)
    ch, cl = split2(
        jnp.concatenate([jnp.concatenate(v, axis=1) for v in (c_all, c_x, c_y)])
    )
    x = mm(jnp.concatenate([ch, ch], axis=1), table[...], NN)
    x = x + mm(cl, table[:WAVES], NN)
    z = zed[...]
    zc, zs = z[:L_ROWS], z[L_ROWS:]
    fz = jnp.sum(
        (x[L_ROWS : 2 * L_ROWS] * zc - x[:L_ROWS] * zs) * l_col, axis=0, keepdims=True
    )
    fx = jnp.sum(x[2 * L_ROWS : 4 * L_ROWS] * z, axis=0, keepdims=True)
    fy = jnp.sum(x[4 * L_ROWS :] * z, axis=0, keepdims=True)
    force = gain[...] * jnp.concatenate([fx, fy, fz * (1.0 / BOX_Z)])
    slot_forces[...] = jnp.where(live, force[:, :slots], 0.0)
    atom_forces[...] = force[:, slots:]

    each(chips, lambda o: ion_copy(o).wait_send())
    each(devices, lambda o: mail_copy(o).wait_send())
    hist_sib_copy().wait_send()
    each(ys, lambda o: hist_copy(o).wait_send())
    sums_copy().wait_send()


def deliver(slot_in, atom_in, slot_forces, atom_forces, sem):
    copies = [
        pltpu.make_async_copy(slot_in, slot_forces, sem.at[0]),
        pltpu.make_async_copy(atom_in, atom_forces, sem.at[1]),
    ]
    for copy in copies:
        copy.start()
    for copy in copies:
        copy.wait()


VMEM = pl.BlockSpec(memory_space=pltpu.VMEM)
HBM = pl.BlockSpec(memory_space=pltpu.HBM)
ANY = pl.BlockSpec(memory_space=pl.ANY)


def body(coords, charges, counts, send_slot, recv_index, wave_ints):
    slots = charges.shape[0]
    atoms = recv_index.shape[0]
    blks, rows = lax.axis_size("blk"), lax.axis_size("row")
    devices = blks * rows
    chips = devices // 2
    cap = 2 * atoms // devices
    scale = FORCE_GAIN / math.sqrt(float(atoms * devices * blks * wave_ints.shape[1]))
    shape = jax.ShapeDtypeStruct
    args = (coords, charges, counts, send_slot, recv_index, wave_ints)
    dma = lambda n: [pltpu.SemaphoreType.DMA((n,))] * 2
    slot_forces, atom_forces = pl.pallas_call(
        functools.partial(kernel, blks, rows, cap, scale),
        out_shape=[pltpu.VMEM((3, slots), F32), pltpu.VMEM((3, atoms), F32)],
        in_specs=[HBM] * 6,
        out_specs=[VMEM] * 2,
        scratch_shapes=[pltpu.VMEM(a.shape, a.dtype) for a in args]
        + [
            pltpu.VMEM((2 * WAVES, slots + atoms), BF16),
            pltpu.VMEM((WAVES, 2 * slots), BF16),
            pltpu.VMEM((WAVES, 2 * slots), BF16),
            pltpu.VMEM((4, slots), F32),
            pltpu.VMEM((chips, 4, slots), F32),
            pltpu.VMEM((devices, 4, 128), F32),
            pltpu.VMEM((devices, 4, 128), F32),
            pltpu.VMEM((H_TILES, 8, 128), F32),
            pltpu.VMEM((H_TILES, 8, 128), F32),
            pltpu.VMEM((H_TILES, 8, 128), F32),
            pltpu.VMEM((blks // 2, H_TILES, 8, 128), F32),
            pltpu.VMEM((2 * L_ROWS, WAVES), F32),
            pltpu.VMEM((T_TILES, 8, 128), F32),
            pltpu.VMEM((T_TILES, 8, 128), F32),
            pltpu.VMEM((2 * L_ROWS, slots + atoms), F32),
            pltpu.VMEM((1, slots + atoms), F32),
            pltpu.VMEM((4 * L_ROWS, QUADS), F32),
            pltpu.VMEM((4 * L_ROWS, slots), BF16),
            pltpu.VMEM((4 * L_ROWS, slots), BF16),
        ]
        + [pltpu.SemaphoreType.DMA((6,))]
        + dma(chips) + dma(devices) + dma(1) + dma(blks // 2) + dma(1),
        compiler_params=pltpu.CompilerParams(
            collective_id=0, has_side_effects=True, vmem_limit_bytes=56 * 2**20
        ),
    )(*args)
    return slot_forces, atom_forces


def solution(mesh):
    ions = P(("groups", "blk", "row"))
    return jax.shard_map(
        body,
        mesh=mesh,
        in_specs=(P(None, *ions), ions, ions, ions, ions, P(None, "blk")),
        out_specs=(P(None, *ions), P(None, *ions)),
        check_vma=False,
    )
```

```python
import functools
import math

import jax
import jax.numpy as jnp
import numpy as np
from jax import lax
from jax.experimental import pallas as pl
from jax.experimental.pallas import tpu as pltpu
from jax.sharding import PartitionSpec as P

EWALD_BETA = 30.0
BOX_Z = 3.0
FORCE_GAIN = 400.0
HMAX = 12
LMAX = 36
L_ROWS = 40
QUADS = 160
REGULAR = HMAX * HMAX
WAVES = 4 * QUADS
W_TILES = WAVES // 128
H_TILES = L_ROWS // 8 * W_TILES
T_TILES = 2 * H_TILES
F32 = jnp.float32
BF16 = jnp.bfloat16
NT = (((1,), (1,)), ((), ()))
NN = (((1,), (0,)), ((), ()))
TWO_PI = 2.0 * math.pi


def fit(f, terms):
    n = 64
    u = 0.125 + 0.125 * np.cos((2 * np.arange(n) + 1) * np.pi / (2 * n))
    c = np.polynomial.chebyshev.Chebyshev.fit(u, f(np.sqrt(u)), terms - 1, domain=[0.0, 0.25])
    return [float(v) for v in c.convert(kind=np.polynomial.Polynomial).coef]


SIN_C = fit(lambda r: np.sin(np.pi * r) / r, 5)
COS_C = fit(lambda r: np.cos(np.pi * r), 5)


def iota(shape, dim):
    return lax.broadcasted_iota(jnp.int32, shape, dim)


def horner(coefs, u):
    out = u * coefs[-1] + coefs[-2]
    for c in coefs[-3::-1]:
        out = out * u + c
    return out


def turns(mult, frac):
    t = mult * frac
    r = t - jnp.floor(t + 0.5)
    u = r * r
    s = r * horner(SIN_C, u)
    c = horner(COS_C, u)
    twice = s + s
    return 1.0 - twice * s, twice * c


def split2(x):
    hi = x.astype(BF16)
    return hi, (x - hi.astype(F32)).astype(BF16)


def split3(x):
    hi = x.astype(BF16)
    rest = x - hi.astype(F32)
    mid = rest.astype(BF16)
    return hi, mid, (rest - mid.astype(F32)).astype(BF16)


def mm(a, b, dims):
    return lax.dot_general(a, b, dims, preferred_element_type=F32)


def mm3(x, picks, dims):
    rows = x.shape[0]
    out = mm(jnp.concatenate(split3(x)), picks, dims)
    return out[:rows] + out[rows : 2 * rows] + out[2 * rows :]


def quad_of(h, k):
    even = jnp.where(k <= 8, 8 * h + k - 9, 83 + 4 * h + k)
    lone = jnp.where(h + k == 0, REGULAR + HMAX, REGULAR - 1 + h + k)
    return jnp.where((h > 0) & (k > 0), even, lone)


def lane_waves():
    lane = iota((1, WAVES), 1)
    block = (lane >> 5) & 3
    quad = ((lane >> 7) << 5) + (lane & 31)
    late = quad - 96
    h = jnp.where(quad < 96, (quad >> 3) + 1, (late >> 2) + 1)
    k = jnp.where(quad < 96, (quad & 7) + 1, (late & 3) + 9)
    lone = jnp.where(quad < REGULAR + HMAX, quad - (REGULAR - 1), 0)
    regular = quad < REGULAR
    odd = (block & 1) == 1
    h = jnp.where(regular, h, jnp.where(odd, 0, lone))
    k = jnp.where(regular, k, jnp.where(odd, lone, 0))
    return h.astype(F32), k.astype(F32), block, regular


def fill_plane(frac_x, frac_y, hi, lo):
    width = frac_x.shape[1]
    row = iota((16, 1), 0)
    mult = jnp.where(row < 12, row + 1, row - 3).astype(F32)
    cx, sx = turns(mult, frac_x)
    cy, sy = turns(mult, frac_y)
    low = iota((8, width), 0) < 4

    def two(v, i):
        a = jnp.broadcast_to(v[i : i + 1], (8, width))
        return jnp.where(low, a, jnp.broadcast_to(v[i + 1 : i + 2], (8, width)))

    def unit(u):
        if u < HMAX:
            a, b = cx[u : u + 1], sx[u : u + 1]
            c, d = cy[:8], sy[:8]
        elif u < 18:
            i = 2 * (u - HMAX)
            a, b = two(cx, i), two(sx, i)
            c, d = cy[8:], sy[8:]
        elif u == 18:
            return cx[:8], cy[:8], sx[:8], sy[:8]
        else:
            return jnp.where(low, cx[8:], 1.0), cy[8:], jnp.where(low, sx[8:], 0.0), sy[8:]
        return a * c, b * d, b * c, a * d

    for t in range(W_TILES):
        units = [unit(4 * t + i) for i in range(4)]
        for block in range(4):
            value = jnp.concatenate([v[block] for v in units])
            place = pl.ds(128 * t + 32 * block, 32)
            hi[place, :], lo[place, :] = split2(value)


def column(frac_z, gain=None):
    c, s = turns((iota((8, 1), 0) + 1).astype(F32), frac_z)
    c8, s8 = c[7:8], s[7:8]
    if gain is not None:
        c, s = c * gain, s * gain
    cs, ss = [c], [s]
    for _ in range(L_ROWS // 8 - 1):
        c, s = c * c8 - s * s8, s * c8 + c * s8
        cs.append(c)
        ss.append(s)
    return jnp.concatenate(cs + ss)


def each(count, f):
    if count <= 16:
        for o in range(1, count):
            f(o)
    else:
        pl.loop(1, count)(f)


def kernel(
    blks, rows, cap, scale,
    coords_in, charges_in, counts_in, send_in, recv_in, wave_in,
    slot_forces, atom_forces,
    coords, charges, counts, send_slot, recv_index, wave,
    table, even, odd, ion, got_ion, mail, got_mail,
    hist, hist_sib, hist_chip, got_hist, acc, sums, from_sib, zed, gain, found, even_v, odd_v,
    in_s, i_s, i_r, m_s, m_r, h_s, h_r, y_s, y_r, x_s, x_r,
):
    devices = blks * rows
    chips = devices // 2
    ys = blks // 2
    slots = coords.shape[1]
    atoms = recv_index.shape[0]
    both = slots + atoms
    blk, row = lax.axis_index("blk"), lax.axis_index("row")
    core = lax.rem(blk, 2)
    y = lax.div(blk, 2)
    me = blk * rows + row
    mesh_id = pl.DeviceIdType.MESH
    sibling = {"blk": blk + 1 - 2 * core, "row": row}

    loads = [
        pltpu.make_async_copy(src, dst, in_s.at[i])
        for i, (src, dst) in enumerate(
            (
                (coords_in, coords), (charges_in, charges), (counts_in, counts),
                (send_in, send_slot), (wave_in, wave), (recv_in, recv_index),
            )
        )
    ]
    for load in loads:
        load.start()

    blk_at = [lax.rem(blk + i, blks) for i in range(blks)]
    row_at = [lax.rem(row + i, rows) for i in range(rows)]

    def other(o):
        if isinstance(o, int):
            return {"blk": blk_at[o // rows], "row": row_at[o % rows]}
        return {"blk": lax.rem(blk + lax.div(o, rows), blks), "row": lax.rem(row + lax.rem(o, rows), rows)}

    def other_chip(o):
        if isinstance(o, int):
            return {"blk": blk_at[2 * (o % ys)], "row": row_at[o // ys]}
        return {"blk": lax.rem(blk + 2 * lax.rem(o, ys), blks), "row": lax.rem(row + lax.div(o, ys), rows)}

    def copy(src, dst, s, r, o, dev):
        return pltpu.make_async_remote_copy(
            src_ref=src, dst_ref=dst, send_sem=s.at[o], recv_sem=r.at[o],
            device_id=dev, device_id_type=mesh_id,
        )

    def ion_copy(o):
        return copy(ion, got_ion.at[o], i_s, i_r, o, other_chip(o))

    def mail_copy(o):
        dev = other(o)
        return copy(mail.at[dev["blk"] * rows + dev["row"]], got_mail.at[o], m_s, m_r, o, dev)

    def hist_sib_copy():
        return copy(hist, hist_sib, h_s, h_r, 0, sibling)

    def hist_copy(o):
        return copy(hist_chip, got_hist.at[o], y_s, y_r, o, other_chip(o))

    def sums_copy():
        return copy(sums, from_sib, x_s, x_r, 0, sibling)

    barrier = pltpu.get_barrier_semaphore()
    each(
        devices,
        lambda o: pl.semaphore_signal(
            barrier, inc=1, device_id=other(o), device_id_type=mesh_id
        ),
    )

    for load in loads[:3]:
        load.wait()
    live = iota((1, slots), 1) < jnp.broadcast_to(counts[...].reshape(1, 1), (1, slots))
    q = jnp.where(live, charges[...].reshape(1, slots), 0.0)
    ion[0:3] = coords[...]
    ion[3:4] = q
    pl.semaphore_wait(barrier, devices - 1)
    each(chips, lambda o: ion_copy(o).start())

    loads[3].wait()
    per_tile = 128 // cap
    target = jnp.where(live, send_slot[...].reshape(1, slots), -cap)
    dest = lax.shift_right_arithmetic(target, cap.bit_length() - 1)
    lane = (target & (cap - 1)) + lax.rem(me, per_tile) * cap
    spots = jnp.where(lane == iota((128, slots), 0), 1.0, 0.0).astype(BF16)
    quad = jnp.concatenate([coords[...], q] * 2)
    terms = [term.astype(F32) for term in split3(quad)]
    half = lax.shift_right_logical(iota((8, slots), 0), 2)
    places = [dest == half + d for d in range(0, devices, 2)]
    rows_of = [
        jnp.where(at, term, 0.0).astype(BF16) for term in terms for at in places
    ]
    out = mm(jnp.concatenate(rows_of), spots, NT)
    n = 4 * devices
    out = out[:n] + out[n : 2 * n] + out[2 * n :]
    for d in range(devices):
        mail[d] = out[4 * d : 4 * d + 4]
    each(devices, lambda o: mail_copy(o).start())

    loads[4].wait()
    k_local = wave.shape[1]
    part = 1536 if k_local % 1536 == 0 else k_local
    found[...] = jnp.zeros_like(found)

    def count(i):
        w = wave[:, pl.ds(pl.multiple_of(i * part, 128), part)]
        h, k, l = w[0:1], w[1:2], w[2:3]
        flip = l < 0
        s1 = jnp.where((h < 0) ^ flip, -1.0, 1.0)
        s2 = jnp.where((k < 0) ^ flip, -1.0, 1.0)
        h, k, l = jnp.abs(h), jnp.abs(k), jnp.abs(l)
        lone_k = (h == 0) & (k > 0)
        s1 = jnp.where(h > 0, s1, 0.0)
        s2 = jnp.where(k > 0, s2, 0.0)
        signs = (
            jnp.where(lone_k, 0.0, 1.0),
            jnp.where(lone_k, 1.0, s1 * s2),
            s1,
            jnp.where(lone_k, -s2, jnp.where(h > 0, s2, 0.0)),
        )
        of_l = l == iota((L_ROWS, part), 0) + 1
        left = jnp.concatenate([jnp.where(of_l, s, 0.0).astype(BF16) for s in signs])
        right = jnp.where(quad_of(h, k) == iota((QUADS, part), 0), 1.0, 0.0).astype(BF16)
        half = part // 2
        found[...] += mm(left[:, :half], right[:, :half], NT) + mm(left[:, half:], right[:, half:], NT)

    pl.loop(0, k_local // part)(count)
    lane_block = iota((L_ROWS, 128), 1) >> 5
    tail = jnp.concatenate([found[:, 128:QUADS]] * 4, axis=1)
    for t in range(W_TILES):
        merged = None
        for c in range(4):
            of_c = (found[:, :128] if t < 4 else tail)[L_ROWS * c : L_ROWS * (c + 1)]
            shift = 32 * (c - t) % 128
            if t < 4 and shift:
                of_c = pltpu.roll(of_c, shift, 1)
            merged = of_c if merged is None else jnp.where(lane_block == c, of_c, merged)
        for i in range(L_ROWS // 8):
            hist[t * (L_ROWS // 8) + i] = merged[8 * i : 8 * i + 8]
    hist_sib_copy().start()

    lanes = lambda part, first, n: table.at[pl.ds(part * WAVES, WAVES), pl.ds(first, n)]
    fill_plane(coords[0:1], coords[1:2], lanes(0, 0, slots), lanes(1, 0, slots))
    z = column(coords[2:3])

    def put(v, value):
        v[: 2 * L_ROWS], v[2 * L_ROWS :] = split2(value)

    def take(o, buf, v):
        put(v, column(got_ion[o, 2:3], got_ion[o, 3:4]))
        fill_plane(got_ion[o, 0:1], got_ion[o, 1:2], buf.at[:, pl.ds(0, slots)], buf.at[:, pl.ds(slots, slots)])

    def add(v, hi, lo):
        acc[...] += mm(hi, v[...], NT)
        acc[:, : 2 * L_ROWS] += mm(lo, v[: 2 * L_ROWS], NT)

    put(even_v, z * q)
    ion_copy(1).wait_recv()
    acc[...] = jnp.zeros_like(acc)
    add(even_v, table[:WAVES, :slots], table[WAVES:, :slots])
    take(1, odd, odd_v)

    hist_sib_copy().wait_recv()
    hist_chip[...] = hist[...] + hist_sib[...]
    each(ys, lambda o: hist_copy(o).start())

    def pair(i):
        o = 2 * i + 2
        ion_copy(o).wait_recv()
        ion_copy(o + 1).wait_recv()
        add(odd_v, odd[:, :slots], odd[:, slots:])
        take(o, even, even_v)
        add(even_v, even[:, :slots], even[:, slots:])
        take(o + 1, odd, odd_v)

    if chips <= 8:

        def rest(_):
            for o in range(2, chips):
                ion_copy(o).wait_recv()
            for o in range(2, chips, 2):
                add(odd_v, odd[:, :slots], odd[:, slots:])
                take(o, even, even_v)
                add(even_v, even[:, :slots], even[:, slots:])
                take(o + 1, odd, odd_v)
            add(odd_v, odd[:, :slots], odd[:, slots:])

        pl.loop(0, 1 + lax.div(blk, blks))(rest)
    else:
        pl.loop(0, chips // 2 - 1)(pair)
        add(odd_v, odd[:, :slots], odd[:, slots:])
    for t in range(W_TILES):
        value = acc[128 * t : 128 * t + 128].T
        value = value[: 2 * L_ROWS] + value[2 * L_ROWS :]
        for i in range(2 * L_ROWS // 8):
            sums[i * W_TILES + t] = value[8 * i : 8 * i + 8]
    sums_copy().start()

    each(devices, lambda o: mail_copy(o).wait_recv())
    got_mail[0] = mail[me]
    arrived = []
    for s in range(devices):
        db = lax.rem(blk - s // rows + blks, blks)
        dr = lax.rem(row - s % rows + rows, rows)
        arrived.append(got_mail[db * rows + dr])
    loads[5].wait()
    index = recv_index[...].reshape(1, atoms)
    rank = index & (cap - 1)
    source = lax.shift_right_logical(index, cap.bit_length() - 1)
    picks = jnp.where(rank == (iota((128, atoms), 0) & (cap - 1)), 1.0, 0.0).astype(BF16)
    came = mm3(jnp.concatenate(arrived), picks, NN)
    half = lax.shift_right_logical(iota((8, atoms), 0), 2)
    ions = jnp.zeros((8, atoms), F32)
    for s in range(0, devices, 2):
        ions = ions + jnp.where(source == half + s, came[4 * s : 4 * s + 8], 0.0)
    ions = ions[:4] + ions[4:]
    fill_plane(ions[0:1], ions[1:2], lanes(0, slots, atoms), lanes(1, slots, atoms))
    zed[:, :slots] = z
    zed[:, slots:] = column(ions[2:3])
    gain[...] = (-scale * TWO_PI) * jnp.concatenate([q, ions[3:4]], axis=1)

    each(ys, lambda o: hist_copy(o).wait_recv())
    times = hist_chip[...]
    for o in range(1, ys):
        times = times + got_hist[o]
    hf, kf, block, regular = lane_waves()
    l_col = (iota((L_ROWS, 1), 0) + 1).astype(F32)
    px, py, pz = TWO_PI * hf, TWO_PI * kf, TWO_PI * l_col / BOX_Z
    k2 = px * px + py * py + pz * pz
    weight = jnp.exp(-k2 / (4.0 * EWALD_BETA * EWALD_BETA)) / k2
    mix = []
    for t in range(W_TILES):
        at = slice(128 * t, 128 * t + 128)
        n = t * (L_ROWS // 8)
        m = jnp.concatenate([times[n + i] for i in range(L_ROWS // 8)]) * weight[:, at]
        rolled = [m] + [pltpu.roll(m, 32 * i, 1) for i in range(1, 4)]
        b = block[:, at]

        def spread(c):
            value = rolled[(3 - c) % 4]
            for n in range(3):
                value = jnp.where(b == n, rolled[(n - c) % 4], value)
            return value

        m0, m1, m2, m3 = (spread(c) for c in range(4))
        if 32 * (t + 1) > REGULAR:
            reg, is_odd = regular[:, at], (b & 1) == 1
            m0, m2 = (
                jnp.where(reg, m0, jnp.where(is_odd, m1, m0)),
                jnp.where(reg, m2, jnp.where(is_odd, m3, m2)),
            )
            m1, m3 = jnp.where(reg, m1, 0.0), jnp.where(reg, m3, 0.0)
        m1 = jnp.where(b < 2, -m1, m1)
        m2 = jnp.where((b == 0) | (b == 3), -m2, m2)
        m3 = jnp.where((b & 1) == 0, -m3, m3)
        mix.append((m0, m1, m2, m3))

    sums_copy().wait_recv()
    c_x, c_y = [], []
    c_all = []
    for t in range(W_TILES):
        at = slice(128 * t, 128 * t + 128)
        b = block[:, at]
        even_b = (b & 1) == 0
        total = jnp.concatenate(
            [sums[i * W_TILES + t] + from_sib[i * W_TILES + t] for i in range(2 * L_ROWS // 8)]
        )
        m0, m1, m2, m3 = mix[t]

        def partners(v):
            r1, r2, r3 = (pltpu.roll(v, 32 * i, 1) for i in range(1, 4))
            return jnp.where(even_b, r3, r1), r2, jnp.where(even_b, r1, r3)

        t1, t2, t3 = partners(total)
        re, im = slice(0, L_ROWS), slice(L_ROWS, 2 * L_ROWS)
        c = jnp.concatenate(
            [
                m0 * total[re] + m1 * t1[re] + m2 * t2[im] + m3 * t3[im],
                m0 * total[im] + m1 * t1[im] - m2 * t2[re] - m3 * t3[re],
            ]
        )
        _, c2, c3 = partners(c)
        h, k, reg = hf[:, at], kf[:, at], regular[:, at]
        c_all.append(c)
        c_x.append(c2 * jnp.where((b == 1) | (b == 2), -h, h))
        k_signed = jnp.where(even_b, k, -k)
        if 32 * (t + 1) > REGULAR:
            lone = jnp.where(b == 1, k, jnp.where(b == 3, -k, 0.0))
            c_y.append(c3 * jnp.where(reg, k_signed, 0.0) + c2 * jnp.where(reg, 0.0, lone))
        else:
            c_y.append(c3 * k_signed)
    ch, cl = split2(
        jnp.concatenate([jnp.concatenate(v, axis=1) for v in (c_all, c_x, c_y)])
    )
    x = mm(jnp.concatenate([ch, ch], axis=1), table[...], NN)
    x = x + mm(cl, table[:WAVES], NN)
    z = zed[...]
    zc, zs = z[:L_ROWS], z[L_ROWS:]
    fz = jnp.sum(
        (x[L_ROWS : 2 * L_ROWS] * zc - x[:L_ROWS] * zs) * l_col, axis=0, keepdims=True
    )
    fx = jnp.sum(x[2 * L_ROWS : 4 * L_ROWS] * z, axis=0, keepdims=True)
    fy = jnp.sum(x[4 * L_ROWS :] * z, axis=0, keepdims=True)
    force = gain[...] * jnp.concatenate([fx, fy, fz * (1.0 / BOX_Z)])
    slot_forces[...] = jnp.where(live, force[:, :slots], 0.0)
    atom_forces[...] = force[:, slots:]

    each(chips, lambda o: ion_copy(o).wait_send())
    each(devices, lambda o: mail_copy(o).wait_send())
    hist_sib_copy().wait_send()
    each(ys, lambda o: hist_copy(o).wait_send())
    sums_copy().wait_send()


def deliver(slot_in, atom_in, slot_forces, atom_forces, sem):
    copies = [
        pltpu.make_async_copy(slot_in, slot_forces, sem.at[0]),
        pltpu.make_async_copy(atom_in, atom_forces, sem.at[1]),
    ]
    for copy in copies:
        copy.start()
    for copy in copies:
        copy.wait()


VMEM = pl.BlockSpec(memory_space=pltpu.VMEM)
HBM = pl.BlockSpec(memory_space=pltpu.HBM)
ANY = pl.BlockSpec(memory_space=pl.ANY)


def body(coords, charges, counts, send_slot, recv_index, wave_ints):
    slots = charges.shape[0]
    atoms = recv_index.shape[0]
    blks, rows = lax.axis_size("blk"), lax.axis_size("row")
    devices = blks * rows
    chips = devices // 2
    cap = 2 * atoms // devices
    scale = FORCE_GAIN / math.sqrt(float(atoms * devices * blks * wave_ints.shape[1]))
    shape = jax.ShapeDtypeStruct
    args = (coords, charges, counts, send_slot, recv_index, wave_ints)
    dma = lambda n: [pltpu.SemaphoreType.DMA((n,))] * 2
    slot_forces, atom_forces = pl.pallas_call(
        functools.partial(kernel, blks, rows, cap, scale),
        out_shape=[pltpu.VMEM((3, slots), F32), pltpu.VMEM((3, atoms), F32)],
        in_specs=[HBM] * 6,
        out_specs=[VMEM] * 2,
        scratch_shapes=[pltpu.VMEM(a.shape, a.dtype) for a in args]
        + [
            pltpu.VMEM((2 * WAVES, slots + atoms), BF16),
            pltpu.VMEM((WAVES, 2 * slots), BF16),
            pltpu.VMEM((WAVES, 2 * slots), BF16),
            pltpu.VMEM((4, slots), F32),
            pltpu.VMEM((chips, 4, slots), F32),
            pltpu.VMEM((devices, 4, 128), F32),
            pltpu.VMEM((devices, 4, 128), F32),
            pltpu.VMEM((H_TILES, 8, 128), F32),
            pltpu.VMEM((H_TILES, 8, 128), F32),
            pltpu.VMEM((H_TILES, 8, 128), F32),
            pltpu.VMEM((blks // 2, H_TILES, 8, 128), F32),
            pltpu.VMEM((WAVES, 4 * L_ROWS), F32),
            pltpu.VMEM((T_TILES, 8, 128), F32),
            pltpu.VMEM((T_TILES, 8, 128), F32),
            pltpu.VMEM((2 * L_ROWS, slots + atoms), F32),
            pltpu.VMEM((1, slots + atoms), F32),
            pltpu.VMEM((4 * L_ROWS, QUADS), F32),
            pltpu.VMEM((4 * L_ROWS, slots), BF16),
            pltpu.VMEM((4 * L_ROWS, slots), BF16),
        ]
        + [pltpu.SemaphoreType.DMA((6,))]
        + dma(chips) + dma(devices) + dma(1) + dma(blks // 2) + dma(1),
        compiler_params=pltpu.CompilerParams(
            collective_id=0, has_side_effects=True, vmem_limit_bytes=56 * 2**20
        ),
    )(*args)
    return slot_forces, atom_forces


def solution(mesh):
    ions = P(("groups", "blk", "row"))
    return jax.shard_map(
        body,
        mesh=mesh,
        in_specs=(P(None, *ions), ions, ions, ions, ions, P(None, "blk")),
        out_specs=(P(None, *ions), P(None, *ions)),
        check_vma=False,
    )
```

```python
import functools
import math

import jax
import jax.numpy as jnp
import numpy as np
from jax import lax
from jax.experimental import pallas as pl
from jax.experimental.pallas import tpu as pltpu
from jax.sharding import PartitionSpec as P

EWALD_BETA = 30.0
BOX_Z = 3.0
FORCE_GAIN = 400.0
HMAX = 12
LMAX = 36
L_ROWS = 40
QUADS = 160
REGULAR = HMAX * HMAX
WAVES = 4 * QUADS
W_TILES = WAVES // 128
H_TILES = L_ROWS // 8 * W_TILES
T_TILES = 2 * H_TILES
F32 = jnp.float32
BF16 = jnp.bfloat16
NT = (((1,), (1,)), ((), ()))
NN = (((1,), (0,)), ((), ()))
TWO_PI = 2.0 * math.pi


def fit(f, terms):
    n = 64
    u = 0.125 + 0.125 * np.cos((2 * np.arange(n) + 1) * np.pi / (2 * n))
    c = np.polynomial.chebyshev.Chebyshev.fit(u, f(np.sqrt(u)), terms - 1, domain=[0.0, 0.25])
    return [float(v) for v in c.convert(kind=np.polynomial.Polynomial).coef]


SIN_C = fit(lambda r: np.sin(np.pi * r) / r, 5)
COS_C = fit(lambda r: np.cos(np.pi * r), 5)


def iota(shape, dim):
    return lax.broadcasted_iota(jnp.int32, shape, dim)


def horner(coefs, u):
    out = u * coefs[-1] + coefs[-2]
    for c in coefs[-3::-1]:
        out = out * u + c
    return out


def turns(mult, frac):
    t = mult * frac
    r = t - jnp.floor(t + 0.5)
    u = r * r
    s = r * horner(SIN_C, u)
    c = horner(COS_C, u)
    twice = s + s
    return 1.0 - twice * s, twice * c


def split2(x):
    hi = x.astype(BF16)
    return hi, (x - hi.astype(F32)).astype(BF16)


def split3(x):
    hi = x.astype(BF16)
    rest = x - hi.astype(F32)
    mid = rest.astype(BF16)
    return hi, mid, (rest - mid.astype(F32)).astype(BF16)


def mm(a, b, dims):
    return lax.dot_general(a, b, dims, preferred_element_type=F32)


def mm3(x, picks, dims):
    rows = x.shape[0]
    out = mm(jnp.concatenate(split3(x)), picks, dims)
    return out[:rows] + out[rows : 2 * rows] + out[2 * rows :]


def quad_of(h, k):
    even = jnp.where(k <= 8, 8 * h + k - 9, 83 + 4 * h + k)
    lone = jnp.where(h + k == 0, REGULAR + HMAX, REGULAR - 1 + h + k)
    return jnp.where((h > 0) & (k > 0), even, lone)


def lane_waves():
    lane = iota((1, WAVES), 1)
    block = (lane >> 5) & 3
    quad = ((lane >> 7) << 5) + (lane & 31)
    late = quad - 96
    h = jnp.where(quad < 96, (quad >> 3) + 1, (late >> 2) + 1)
    k = jnp.where(quad < 96, (quad & 7) + 1, (late & 3) + 9)
    lone = jnp.where(quad < REGULAR + HMAX, quad - (REGULAR - 1), 0)
    regular = quad < REGULAR
    odd = (block & 1) == 1
    h = jnp.where(regular, h, jnp.where(odd, 0, lone))
    k = jnp.where(regular, k, jnp.where(odd, lone, 0))
    return h.astype(F32), k.astype(F32), block, regular


def fill_plane(frac_x, frac_y, hi, lo):
    width = frac_x.shape[1]
    row = iota((16, 1), 0)
    mult = jnp.where(row < 12, row + 1, row - 3).astype(F32)
    cx, sx = turns(mult, frac_x)
    cy, sy = turns(mult, frac_y)
    low = iota((8, width), 0) < 4

    def two(v, i):
        a = jnp.broadcast_to(v[i : i + 1], (8, width))
        return jnp.where(low, a, jnp.broadcast_to(v[i + 1 : i + 2], (8, width)))

    def unit(u):
        if u < HMAX:
            a, b = cx[u : u + 1], sx[u : u + 1]
            c, d = cy[:8], sy[:8]
        elif u < 18:
            i = 2 * (u - HMAX)
            a, b = two(cx, i), two(sx, i)
            c, d = cy[8:], sy[8:]
        elif u == 18:
            return cx[:8], cy[:8], sx[:8], sy[:8]
        else:
            return jnp.where(low, cx[8:], 1.0), cy[8:], jnp.where(low, sx[8:], 0.0), sy[8:]
        return a * c, b * d, b * c, a * d

    for t in range(W_TILES):
        units = [unit(4 * t + i) for i in range(4)]
        for block in range(4):
            value = jnp.concatenate([v[block] for v in units])
            place = pl.ds(128 * t + 32 * block, 32)
            hi[place, :], lo[place, :] = split2(value)


def column(frac_z, gain=None):
    c, s = turns((iota((8, 1), 0) + 1).astype(F32), frac_z)
    c8, s8 = c[7:8], s[7:8]
    if gain is not None:
        c, s = c * gain, s * gain
    cs, ss = [c], [s]
    for _ in range(L_ROWS // 8 - 1):
        c, s = c * c8 - s * s8, s * c8 + c * s8
        cs.append(c)
        ss.append(s)
    return jnp.concatenate(cs + ss)


def each(count, f):
    if count <= 16:
        for o in range(1, count):
            f(o)
    else:
        pl.loop(1, count)(f)


def kernel(
    blks, rows, cap, scale,
    coords_in, charges_in, counts_in, send_in, recv_in, wave_in,
    slot_forces, atom_forces,
    coords, charges, counts, send_slot, recv_index, wave,
    table, even, odd, ion, got_ion, mail, got_mail,
    hist, hist_sib, hist_chip, got_hist, acc, sums, from_sib, zed, gain, found, even_v, odd_v,
    in_s, i_s, i_r, m_s, m_r, h_s, h_r, y_s, y_r, x_s, x_r,
):
    devices = blks * rows
    chips = devices // 2
    ys = blks // 2
    slots = coords.shape[1]
    atoms = recv_index.shape[0]
    both = slots + atoms
    blk, row = lax.axis_index("blk"), lax.axis_index("row")
    core = lax.rem(blk, 2)
    y = lax.div(blk, 2)
    me = blk * rows + row
    mesh_id = pl.DeviceIdType.MESH
    sibling = {"blk": blk + 1 - 2 * core, "row": row}

    loads = [
        pltpu.make_async_copy(src, dst, in_s.at[i])
        for i, (src, dst) in enumerate(
            (
                (coords_in, coords), (charges_in, charges), (counts_in, counts),
                (send_in, send_slot), (wave_in, wave), (recv_in, recv_index),
            )
        )
    ]
    for load in loads:
        load.start()

    blk_at = [lax.rem(blk + i, blks) for i in range(blks)]
    row_at = [lax.rem(row + i, rows) for i in range(rows)]

    def other(o):
        if isinstance(o, int):
            return {"blk": blk_at[o // rows], "row": row_at[o % rows]}
        return {"blk": lax.rem(blk + lax.div(o, rows), blks), "row": lax.rem(row + lax.rem(o, rows), rows)}

    def other_chip(o):
        if isinstance(o, int):
            return {"blk": blk_at[2 * (o % ys)], "row": row_at[o // ys]}
        return {"blk": lax.rem(blk + 2 * lax.rem(o, ys), blks), "row": lax.rem(row + lax.div(o, ys), rows)}

    def copy(src, dst, s, r, o, dev):
        return pltpu.make_async_remote_copy(
            src_ref=src, dst_ref=dst, send_sem=s.at[o], recv_sem=r.at[o],
            device_id=dev, device_id_type=mesh_id,
        )

    def ion_copy(o):
        return copy(ion, got_ion.at[o], i_s, i_r, o, other_chip(o))

    def mail_copy(o):
        dev = other(o)
        return copy(mail.at[dev["blk"] * rows + dev["row"]], got_mail.at[o], m_s, m_r, o, dev)

    def hist_sib_copy():
        return copy(hist, hist_sib, h_s, h_r, 0, sibling)

    def hist_copy(o):
        return copy(hist_chip, got_hist.at[o], y_s, y_r, o, other_chip(o))

    def sums_copy():
        return copy(sums, from_sib, x_s, x_r, 0, sibling)

    barrier = pltpu.get_barrier_semaphore()
    each(
        devices,
        lambda o: pl.semaphore_signal(
            barrier, inc=1, device_id=other(o), device_id_type=mesh_id
        ),
    )

    for load in loads[:3]:
        load.wait()
    live = iota((1, slots), 1) < jnp.broadcast_to(counts[...].reshape(1, 1), (1, slots))
    q = jnp.where(live, charges[...].reshape(1, slots), 0.0)
    ion[0:3] = coords[...]
    ion[3:4] = q
    pl.semaphore_wait(barrier, devices - 1)
    each(chips, lambda o: ion_copy(o).start())

    loads[3].wait()
    per_tile = 128 // cap
    target = jnp.where(live, send_slot[...].reshape(1, slots), -cap)
    dest = lax.shift_right_arithmetic(target, cap.bit_length() - 1)
    lane = (target & (cap - 1)) + lax.rem(me, per_tile) * cap
    spots = jnp.where(lane == iota((128, slots), 0), 1.0, 0.0).astype(BF16)
    quad = jnp.concatenate([coords[...], q] * 2)
    terms = [term.astype(F32) for term in split3(quad)]
    half = lax.shift_right_logical(iota((8, slots), 0), 2)
    places = [dest == half + d for d in range(0, devices, 2)]
    rows_of = [
        jnp.where(at, term, 0.0).astype(BF16) for term in terms for at in places
    ]
    out = mm(jnp.concatenate(rows_of), spots, NT)
    n = 4 * devices
    out = out[:n] + out[n : 2 * n] + out[2 * n :]
    for d in range(devices):
        mail[d] = out[4 * d : 4 * d + 4]
    each(devices, lambda o: mail_copy(o).start())

    loads[4].wait()
    k_local = wave.shape[1]
    part = 3072 if k_local % 3072 == 0 else k_local
    found[...] = jnp.zeros_like(found)

    def count(i):
        w = wave[:, pl.ds(pl.multiple_of(i * part, 128), part)]
        h, k, l = w[0:1], w[1:2], w[2:3]
        flip = l < 0
        s1 = jnp.where((h < 0) ^ flip, -1.0, 1.0)
        s2 = jnp.where((k < 0) ^ flip, -1.0, 1.0)
        h, k, l = jnp.abs(h), jnp.abs(k), jnp.abs(l)
        lone_k = (h == 0) & (k > 0)
        s1 = jnp.where(h > 0, s1, 0.0)
        s2 = jnp.where(k > 0, s2, 0.0)
        signs = (
            jnp.where(lone_k, 0.0, 1.0),
            jnp.where(lone_k, 1.0, s1 * s2),
            s1,
            jnp.where(lone_k, -s2, jnp.where(h > 0, s2, 0.0)),
        )
        of_l = l == iota((L_ROWS, part), 0) + 1
        left = jnp.concatenate([jnp.where(of_l, s, 0.0).astype(BF16) for s in signs])
        right = jnp.where(quad_of(h, k) == iota((QUADS, part), 0), 1.0, 0.0).astype(BF16)
        half = part // 2
        found[...] += mm(left[:, :half], right[:, :half], NT) + mm(left[:, half:], right[:, half:], NT)

    pl.loop(0, k_local // part)(count)
    lane_block = iota((L_ROWS, 128), 1) >> 5
    tail = jnp.concatenate([found[:, 128:QUADS]] * 4, axis=1)
    for t in range(W_TILES):
        merged = None
        for c in range(4):
            of_c = (found[:, :128] if t < 4 else tail)[L_ROWS * c : L_ROWS * (c + 1)]
            shift = 32 * (c - t) % 128
            if t < 4 and shift:
                of_c = pltpu.roll(of_c, shift, 1)
            merged = of_c if merged is None else jnp.where(lane_block == c, of_c, merged)
        for i in range(L_ROWS // 8):
            hist[t * (L_ROWS // 8) + i] = merged[8 * i : 8 * i + 8]
    hist_sib_copy().start()

    lanes = lambda part, first, n: table.at[pl.ds(part * WAVES, WAVES), pl.ds(first, n)]
    fill_plane(coords[0:1], coords[1:2], lanes(0, 0, slots), lanes(1, 0, slots))
    z = column(coords[2:3])

    def put(v, value):
        v[: 2 * L_ROWS], v[2 * L_ROWS :] = split2(value)

    def take(o, buf, v):
        put(v, column(got_ion[o, 2:3], got_ion[o, 3:4]))
        fill_plane(got_ion[o, 0:1], got_ion[o, 1:2], buf.at[:, pl.ds(0, slots)], buf.at[:, pl.ds(slots, slots)])

    def add(v, hi, lo):
        acc[...] += mm(hi, v[...], NT)
        acc[:, : 2 * L_ROWS] += mm(lo, v[: 2 * L_ROWS], NT)

    put(even_v, z * q)
    ion_copy(1).wait_recv()
    acc[...] = jnp.zeros_like(acc)
    add(even_v, table[:WAVES, :slots], table[WAVES:, :slots])
    take(1, odd, odd_v)

    hist_sib_copy().wait_recv()
    hist_chip[...] = hist[...] + hist_sib[...]
    each(ys, lambda o: hist_copy(o).start())

    def pair(i):
        o = 2 * i + 2
        ion_copy(o).wait_recv()
        ion_copy(o + 1).wait_recv()
        add(odd_v, odd[:, :slots], odd[:, slots:])
        take(o, even, even_v)
        add(even_v, even[:, :slots], even[:, slots:])
        take(o + 1, odd, odd_v)

    if chips <= 8:

        def rest(_):
            for o in range(2, chips):
                ion_copy(o).wait_recv()
            for o in range(2, chips, 2):
                add(odd_v, odd[:, :slots], odd[:, slots:])
                take(o, even, even_v)
                add(even_v, even[:, :slots], even[:, slots:])
                take(o + 1, odd, odd_v)
            add(odd_v, odd[:, :slots], odd[:, slots:])

        pl.loop(0, 1 + lax.div(blk, blks))(rest)
    else:
        pl.loop(0, chips // 2 - 1)(pair)
        add(odd_v, odd[:, :slots], odd[:, slots:])
    for t in range(W_TILES):
        value = acc[128 * t : 128 * t + 128].T
        value = value[: 2 * L_ROWS] + value[2 * L_ROWS :]
        for i in range(2 * L_ROWS // 8):
            sums[i * W_TILES + t] = value[8 * i : 8 * i + 8]
    sums_copy().start()

    each(devices, lambda o: mail_copy(o).wait_recv())
    got_mail[0] = mail[me]
    arrived = []
    for s in range(devices):
        db = lax.rem(blk - s // rows + blks, blks)
        dr = lax.rem(row - s % rows + rows, rows)
        arrived.append(got_mail[db * rows + dr])
    loads[5].wait()
    index = recv_index[...].reshape(1, atoms)
    rank = index & (cap - 1)
    source = lax.shift_right_logical(index, cap.bit_length() - 1)
    picks = jnp.where(rank == (iota((128, atoms), 0) & (cap - 1)), 1.0, 0.0).astype(BF16)
    came = mm3(jnp.concatenate(arrived), picks, NN)
    half = lax.shift_right_logical(iota((8, atoms), 0), 2)
    ions = jnp.zeros((8, atoms), F32)
    for s in range(0, devices, 2):
        ions = ions + jnp.where(source == half + s, came[4 * s : 4 * s + 8], 0.0)
    ions = ions[:4] + ions[4:]
    fill_plane(ions[0:1], ions[1:2], lanes(0, slots, atoms), lanes(1, slots, atoms))
    zed[:, :slots] = z
    zed[:, slots:] = column(ions[2:3])
    gain[...] = (-scale * TWO_PI) * jnp.concatenate([q, ions[3:4]], axis=1)

    each(ys, lambda o: hist_copy(o).wait_recv())
    times = hist_chip[...]
    for o in range(1, ys):
        times = times + got_hist[o]
    hf, kf, block, regular = lane_waves()
    l_col = (iota((L_ROWS, 1), 0) + 1).astype(F32)
    px, py, pz = TWO_PI * hf, TWO_PI * kf, TWO_PI * l_col / BOX_Z
    k2 = px * px + py * py + pz * pz
    weight = jnp.exp(-k2 / (4.0 * EWALD_BETA * EWALD_BETA)) / k2
    mix = []
    for t in range(W_TILES):
        at = slice(128 * t, 128 * t + 128)
        n = t * (L_ROWS // 8)
        m = jnp.concatenate([times[n + i] for i in range(L_ROWS // 8)]) * weight[:, at]
        rolled = [m] + [pltpu.roll(m, 32 * i, 1) for i in range(1, 4)]
        b = block[:, at]

        def spread(c):
            value = rolled[(3 - c) % 4]
            for n in range(3):
                value = jnp.where(b == n, rolled[(n - c) % 4], value)
            return value

        m0, m1, m2, m3 = (spread(c) for c in range(4))
        if 32 * (t + 1) > REGULAR:
            reg, is_odd = regular[:, at], (b & 1) == 1
            m0, m2 = (
                jnp.where(reg, m0, jnp.where(is_odd, m1, m0)),
                jnp.where(reg, m2, jnp.where(is_odd, m3, m2)),
            )
            m1, m3 = jnp.where(reg, m1, 0.0), jnp.where(reg, m3, 0.0)
        m1 = jnp.where(b < 2, -m1, m1)
        m2 = jnp.where((b == 0) | (b == 3), -m2, m2)
        m3 = jnp.where((b & 1) == 0, -m3, m3)
        mix.append((m0, m1, m2, m3))

    sums_copy().wait_recv()
    c_x, c_y = [], []
    c_all = []
    for t in range(W_TILES):
        at = slice(128 * t, 128 * t + 128)
        b = block[:, at]
        even_b = (b & 1) == 0
        total = jnp.concatenate(
            [sums[i * W_TILES + t] + from_sib[i * W_TILES + t] for i in range(2 * L_ROWS // 8)]
        )
        m0, m1, m2, m3 = mix[t]

        def partners(v):
            r1, r2, r3 = (pltpu.roll(v, 32 * i, 1) for i in range(1, 4))
            return jnp.where(even_b, r3, r1), r2, jnp.where(even_b, r1, r3)

        t1, t2, t3 = partners(total)
        re, im = slice(0, L_ROWS), slice(L_ROWS, 2 * L_ROWS)
        c = jnp.concatenate(
            [
                m0 * total[re] + m1 * t1[re] + m2 * t2[im] + m3 * t3[im],
                m0 * total[im] + m1 * t1[im] - m2 * t2[re] - m3 * t3[re],
            ]
        )
        _, c2, c3 = partners(c)
        h, k, reg = hf[:, at], kf[:, at], regular[:, at]
        c_all.append(c)
        c_x.append(c2 * jnp.where((b == 1) | (b == 2), -h, h))
        k_signed = jnp.where(even_b, k, -k)
        if 32 * (t + 1) > REGULAR:
            lone = jnp.where(b == 1, k, jnp.where(b == 3, -k, 0.0))
            c_y.append(c3 * jnp.where(reg, k_signed, 0.0) + c2 * jnp.where(reg, 0.0, lone))
        else:
            c_y.append(c3 * k_signed)
    ch, cl = split2(
        jnp.concatenate([jnp.concatenate(v, axis=1) for v in (c_all, c_x, c_y)])
    )
    x = mm(jnp.concatenate([ch, ch], axis=1), table[...], NN)
    x = x + mm(cl, table[:WAVES], NN)
    z = zed[...]
    zc, zs = z[:L_ROWS], z[L_ROWS:]
    fz = jnp.sum(
        (x[L_ROWS : 2 * L_ROWS] * zc - x[:L_ROWS] * zs) * l_col, axis=0, keepdims=True
    )
    fx = jnp.sum(x[2 * L_ROWS : 4 * L_ROWS] * z, axis=0, keepdims=True)
    fy = jnp.sum(x[4 * L_ROWS :] * z, axis=0, keepdims=True)
    force = gain[...] * jnp.concatenate([fx, fy, fz * (1.0 / BOX_Z)])
    slot_forces[...] = jnp.where(live, force[:, :slots], 0.0)
    atom_forces[...] = force[:, slots:]

    each(chips, lambda o: ion_copy(o).wait_send())
    each(devices, lambda o: mail_copy(o).wait_send())
    hist_sib_copy().wait_send()
    each(ys, lambda o: hist_copy(o).wait_send())
    sums_copy().wait_send()


def deliver(slot_in, atom_in, slot_forces, atom_forces, sem):
    copies = [
        pltpu.make_async_copy(slot_in, slot_forces, sem.at[0]),
        pltpu.make_async_copy(atom_in, atom_forces, sem.at[1]),
    ]
    for copy in copies:
        copy.start()
    for copy in copies:
        copy.wait()


VMEM = pl.BlockSpec(memory_space=pltpu.VMEM)
HBM = pl.BlockSpec(memory_space=pltpu.HBM)
ANY = pl.BlockSpec(memory_space=pl.ANY)


def body(coords, charges, counts, send_slot, recv_index, wave_ints):
    slots = charges.shape[0]
    atoms = recv_index.shape[0]
    blks, rows = lax.axis_size("blk"), lax.axis_size("row")
    devices = blks * rows
    chips = devices // 2
    cap = 2 * atoms // devices
    scale = FORCE_GAIN / math.sqrt(float(atoms * devices * blks * wave_ints.shape[1]))
    shape = jax.ShapeDtypeStruct
    args = (coords, charges, counts, send_slot, recv_index, wave_ints)
    dma = lambda n: [pltpu.SemaphoreType.DMA((n,))] * 2
    slot_forces, atom_forces = pl.pallas_call(
        functools.partial(kernel, blks, rows, cap, scale),
        out_shape=[pltpu.VMEM((3, slots), F32), pltpu.VMEM((3, atoms), F32)],
        in_specs=[HBM] * 6,
        out_specs=[VMEM] * 2,
        scratch_shapes=[pltpu.VMEM(a.shape, a.dtype) for a in args]
        + [
            pltpu.VMEM((2 * WAVES, slots + atoms), BF16),
            pltpu.VMEM((WAVES, 2 * slots), BF16),
            pltpu.VMEM((WAVES, 2 * slots), BF16),
            pltpu.VMEM((4, slots), F32),
            pltpu.VMEM((chips, 4, slots), F32),
            pltpu.VMEM((devices, 4, 128), F32),
            pltpu.VMEM((devices, 4, 128), F32),
            pltpu.VMEM((H_TILES, 8, 128), F32),
            pltpu.VMEM((H_TILES, 8, 128), F32),
            pltpu.VMEM((H_TILES, 8, 128), F32),
            pltpu.VMEM((blks // 2, H_TILES, 8, 128), F32),
            pltpu.VMEM((WAVES, 4 * L_ROWS), F32),
            pltpu.VMEM((T_TILES, 8, 128), F32),
            pltpu.VMEM((T_TILES, 8, 128), F32),
            pltpu.VMEM((2 * L_ROWS, slots + atoms), F32),
            pltpu.VMEM((1, slots + atoms), F32),
            pltpu.VMEM((4 * L_ROWS, QUADS), F32),
            pltpu.VMEM((4 * L_ROWS, slots), BF16),
            pltpu.VMEM((4 * L_ROWS, slots), BF16),
        ]
        + [pltpu.SemaphoreType.DMA((6,))]
        + dma(chips) + dma(devices) + dma(1) + dma(blks // 2) + dma(1),
        compiler_params=pltpu.CompilerParams(
            collective_id=0, has_side_effects=True, vmem_limit_bytes=56 * 2**20
        ),
    )(*args)
    return slot_forces, atom_forces


def solution(mesh):
    ions = P(("groups", "blk", "row"))
    return jax.shard_map(
        body,
        mesh=mesh,
        in_specs=(P(None, *ions), ions, ions, ions, ions, P(None, "blk")),
        out_specs=(P(None, *ions), P(None, *ions)),
        check_vma=False,
    )
```
